512 devices in a mesh: row: 16 (over y, x_hi, core), col: 32 (over z, x_lo).
Axes of the slice: x: 4 (x_hi: 2, x_lo: 2; x = x_hi * 2 + x_lo), y: 4, z: 16, core: 2. Of those that a mesh axis runs over, the one named last changes fastest.
Arguments:
- queries: bfloat16 [65536, 32, 128], P(('col', 'row')), may hold values from -100 to 100
- rotated_key_rows: bfloat16 [65536, 4, 128], P(('col', 'row')), may hold values from -6 to 6
- value_matrix_rows: bfloat16 [65536, 4, 128], P(('col', 'row')), may hold values from -6 to 6
- doc_start: int32 [65536], P(('col', 'row')), may hold values from 0 to 65535, as said below
- block_keep: int32 [512, 512], P(('col', 'row')), may hold values 0 or 1
Outputs:
- attention_out: bfloat16 [65536, 32, 128], P(('col', 'row'))
The draws below stay inside these ranges and needn't reach their ends.
Inputs may be any that keep to these rules, and one draw needn't show every extreme that they name: doc_start[p] is the first position of the document that holds token p; documents are runs of consecutive positions of 1 to 2048 tokens, and at least one holds exactly 2048.
All inputs are finite; a program needn't handle non-finite values. No bound on the sum of `block_keep` on one device may be relied on, other than what follows from the above.
Results may differ from the reference program's by a relative error of at most 0.005.
Values may be sent and summed in bfloat16 or wider, within the bound.
A program may use at most 64 MiB of HBM per device.

```python
import math
import jax
import jax.numpy as jnp
from jax import lax

HEAD_SIZE = 128
QUERY_HEAD_COUNT = 32
KEY_VALUE_HEADS = 4
BLOCK_TOKENS = 128
QUERY_PER_KEY = 8
NB = 512
TOKEN_COUNT = 65536
DOCUMENT_LENGTH = 2048


def draw_queries(key, part):
    key = jax.random.fold_in(key, 1)
    random_jitter = jax.random.normal(key, (TOKEN_COUNT, QUERY_HEAD_COUNT, HEAD_SIZE), jnp.float32)
    return jnp.clip(random_jitter, -6.0, 6.0).astype(jnp.bfloat16)


def draw_rotated_key_rows(key, part):
    key = jax.random.fold_in(key, 2)
    random_jitter = jnp.clip(jax.random.normal(key, (TOKEN_COUNT, KEY_VALUE_HEADS, HEAD_SIZE), jnp.float32), -6.0, 6.0)
    return random_jitter.astype(jnp.bfloat16)


def draw_doc_start(key, part):
    key = jax.random.fold_in(key, 3)
    shortest = max(1, DOCUMENT_LENGTH // 16)
    doc_count = TOKEN_COUNT // shortest + 2
    lengths = jax.random.randint(key, (doc_count,), shortest, DOCUMENT_LENGTH + 1, dtype=jnp.int32)
    lengths = lengths.at[1].set(DOCUMENT_LENGTH)
    doc_starts = jnp.cumsum(lengths) - lengths
    position = jnp.arange(TOKEN_COUNT, dtype=jnp.int32)
    owner = jnp.searchsorted(doc_starts, position, side='right') - 1
    return doc_starts[owner].astype(jnp.int32)


def set_ends(drawn, key, least, top_value):
    longest = drawn.shape.index(max(drawn.shape))
    spots = []
    for shift in (0, 1):
        where = [jax.random.randint(jax.random.fold_in(key, axis), (), 0, length) for axis, length in enumerate(drawn.shape)]
        where[longest] = (where[longest] + shift) % drawn.shape[longest]
        spots.append(tuple(where))
    return drawn.at[spots[0]].set(least).at[spots[1]].set(top_value)


def steps_of(stream_key, shape, cuts, smallest, largest):
    loudness, own = 1.0, jax.random.fold_in(stream_key, 6)
    for dim, shards_of in cuts:
        steps = jnp.exp(jax.random.uniform(jax.random.fold_in(own, dim), (shards_of,), jnp.float32, smallest / len(cuts), largest / len(cuts)))
        loudness = loudness * jnp.repeat(steps, shape[dim] // shards_of).reshape([-1 if axis == dim else 1 for axis in range(len(shape))])
    return loudness


def noise(rng, extent, spread, most, shards=(), held_as=jnp.bfloat16):
    values = jax.random.normal(rng, extent, jnp.float32) * spread
    if len(shards) > 0:
        values = steps_of(rng, extent, shards, -0.22, 0.18) * values
    return jnp.clip(values, min=-most, max=most).astype(held_as)


def setup_inputs(seed: int = 0) -> dict:
    key_list = jax.random.split(jax.random.key(seed), 6)
    return {
        "queries": draw_queries(jax.random.fold_in(key_list[5], 71), 0),
        "rotated_key_rows": draw_rotated_key_rows(jax.random.fold_in(key_list[5], 71), 0),
        "value_matrix_rows": noise(key_list[2], (TOKEN_COUNT, KEY_VALUE_HEADS, HEAD_SIZE), 1.0, 6.0, ((0, 512),)),
        "doc_start": draw_doc_start(jax.random.fold_in(key_list[5], 71), 0),
        "block_keep": set_ends((jax.random.randint(key_list[4], (NB, NB), 0, 4) < 3).astype(jnp.int32), jax.random.fold_in(key_list[4], 1), 0, 1),
    }


NEGATIVE_FILL = -1e+30

def reference(queries, rotated_key_rows, value_matrix_rows, doc_start, block_keep):
    score_scale = 1.0 / math.sqrt(HEAD_SIZE)
    padded_keys = jnp.concatenate([jnp.zeros((DOCUMENT_LENGTH, KEY_VALUE_HEADS, HEAD_SIZE), rotated_key_rows.dtype), rotated_key_rows], axis=0)
    padded_values = jnp.concatenate([jnp.zeros((DOCUMENT_LENGTH, KEY_VALUE_HEADS, HEAD_SIZE), value_matrix_rows.dtype), value_matrix_rows], axis=0)
    start_pad = jnp.concatenate([jnp.full((DOCUMENT_LENGTH,), -1, jnp.int32), doc_start.astype(jnp.int32)], axis=0)

    def one_block(number):
        first = (number * BLOCK_TOKENS).astype(jnp.int32)
        block_queries = lax.dynamic_slice_in_dim(queries, first, BLOCK_TOKENS, 0)
        block_queries = block_queries.astype(jnp.float32).reshape(BLOCK_TOKENS, KEY_VALUE_HEADS, QUERY_PER_KEY, HEAD_SIZE)
        query_starts = lax.dynamic_slice_in_dim(doc_start.astype(jnp.int32), first, BLOCK_TOKENS, 0)
        key_block = lax.dynamic_slice_in_dim(padded_keys, first, DOCUMENT_LENGTH + BLOCK_TOKENS, 0).astype(jnp.float32)
        value_block = lax.dynamic_slice_in_dim(padded_values, first, DOCUMENT_LENGTH + BLOCK_TOKENS, 0).astype(jnp.float32)
        key_starts = lax.dynamic_slice_in_dim(start_pad, first, DOCUMENT_LENGTH + BLOCK_TOKENS, 0)
        key_pos = first - DOCUMENT_LENGTH + jnp.arange(DOCUMENT_LENGTH + BLOCK_TOKENS, dtype=jnp.int32)
        query_pos = first + jnp.arange(BLOCK_TOKENS, dtype=jnp.int32)
        key_owner = key_pos // BLOCK_TOKENS
        keep_row = block_keep[number]
        keep_tok = keep_row[jnp.clip(key_owner, 0, NB - 1)]
        allowed = (keep_tok == 1) | (key_owner == number)
        visible = (query_starts[:, None] == key_starts[None, :]) & (key_pos[None, :] <= query_pos[:, None])
        visible = visible & allowed[None, :] & (key_pos[None, :] >= 0)
        scores = jnp.einsum('qhgd,khd->hgqk', block_queries, key_block) * score_scale
        row_max = lax.optimization_barrier(jnp.max(jnp.where(visible, scores, NEGATIVE_FILL), axis=-1))
        weights = jnp.where(visible, jnp.exp(scores - row_max[..., None]), 0.0)
        weight_total = lax.optimization_barrier(jnp.sum(weights, axis=-1))
        rounded = weights.astype(jnp.bfloat16)
        attended = jnp.einsum('hgqk,khd->hgqd', rounded.astype(jnp.float32), value_block)
        result = attended / weight_total[..., None]
        return result.transpose(2, 0, 1, 3).reshape(BLOCK_TOKENS, QUERY_HEAD_COUNT, HEAD_SIZE).astype(jnp.bfloat16)
    blocks_out = lax.map(one_block, jnp.arange(NB, dtype=jnp.int32))
    return blocks_out.reshape(TOKEN_COUNT, QUERY_HEAD_COUNT, HEAD_SIZE)
```

```python
import functools
import math

import jax
import jax.numpy as jnp
from jax import lax
from jax.experimental import pallas as pl
from jax.experimental.pallas import tpu as pltpu
from jax.sharding import PartitionSpec as P

MASKED = -1e30
STAGES = ((0,), (1, 2), (3, 4), (5, 6), (7, 8))
OFFSETS = (1, 3, 2)
CHUNKS = 9
TILE = 512
F32, BF16 = jnp.float32, jnp.bfloat16


def kernel(rows, cols, q_hbm, kv_ref, start_ref, keep_ref, out_hbm,
           kvbuf, kvs, qraw, meta, qbuf, hot, bias, acc, top, ostage,
           one_send, one_recv, two_send, two_recv, mate_send, mate_recv, here):
    block = q_hbm.shape[0]
    per_seg = rows // 2
    ring = per_seg // 2
    row, col = lax.axis_index("row"), lax.axis_index("col")
    core = lax.rem(row, 2)
    other = 1 - core
    place = row // 2
    side = lax.rem(place, 2)
    y = place // 2
    chip = col * per_seg + place
    next_col = lax.rem(col + 1, cols)
    last_col = lax.rem(col + cols - 1, cols)

    def device(seg, at_y, at_side, which):
        return {"row": (at_y * 2 + at_side) * 2 + which, "col": seg}

    mate = device(col, y, side, other)

    def remote(src, dst, send, recv, target):
        return pltpu.make_async_remote_copy(
            src_ref=src, dst_ref=dst, send_sem=send, recv_sem=recv,
            device_id=target, device_id_type=pl.DeviceIdType.MESH)

    def arrived(dst, sem):
        remote(dst, dst, mate_send.at[0], sem, mate).wait_recv()

    barrier = pltpu.get_barrier_semaphore()

    def greet(target):
        pl.semaphore_signal(barrier, inc=1, device_id=target, device_id_type=pl.DeviceIdType.MESH)

    greet(mate)
    for which in (0, 1):
        greet(device(col, y, 1 - side, which))
        greet(device(last_col, y, side, which))
        greet(device(last_col, y, 1 - side, which))
    for offset in OFFSETS:
        greet(device(col, lax.rem(y + offset, ring), side, core))

    def half(which):
        return pl.ds(pl.multiple_of(which * 16, 16), 16)

    own_q = pltpu.make_async_copy(q_hbm.at[:, half(core), :], qraw.at[core], here.at[0])
    own_q.start()

    for which in (0, 1):
        for h in (0, 1):
            kvs[which, 0, h] = kv_ref[which, 0, h].astype(F32).T.astype(BF16)
            kvs[which, 1, h] = kv_ref[which, 1, h]
    own_kv = pltpu.make_async_copy(kvs.at[core], kvbuf.at[0, core], here.at[1])
    own_kv.start()

    backs = [0, 7 - 6 * side, 8]
    slots = [0, 3 - 2 * side, 2]
    for place_at, offset in enumerate(OFFSETS):
        backs += [2 * offset, 2 * offset - 1 + 2 * side]
        slots += [4 + 2 * place_at, 5 + 2 * place_at]

    own_block = chip * 2 + core
    for i in range(CHUNKS):
        for which in (0, 1):
            number = (chip - backs[i]) * 2 + which
            flag = keep_ref[0, jnp.maximum(number, 0)]
            flag = jnp.where(number == own_block, 1, flag)
            line = i * 2 + which
            meta[core, line:line + 1, :] = jnp.full((1, block), flag, jnp.int32)
    line = 2 * CHUNKS
    meta[core, line:line + 1, :] = start_ref[...]

    pl.semaphore_wait(barrier, 10)

    sends = [
        remote(kvs.at[other], kvbuf.at[0, core], mate_send.at[2], mate_recv.at[2], mate),
        remote(meta.at[core], meta.at[core], mate_send.at[0], mate_recv.at[0], mate),
        remote(q_hbm.at[:, half(other), :], qraw.at[core], mate_send.at[1], mate_recv.at[1], mate),
    ]
    for slot, seg, at_side in ((2, next_col, side), (1, col, 1 - side), (3, next_col, 1 - side)):
        for which in (0, 1):
            sends.append(remote(kvs.at[which], kvbuf.at[slot, core],
                                one_send.at[slot - 1, which], one_recv.at[slot - 1, core],
                                device(seg, y, at_side, which)))
    for send in sends:
        send.start()

    def along(i, offset, cross):
        held = y + offset < ring
        source = jnp.where(held, 0, 2) + cross
        to = 4 + 2 * i + cross
        return remote(kvbuf.at[source], kvbuf.at[to], two_send.at[i, cross], two_recv.at[i, cross],
                      device(col, lax.rem(y + offset, ring), side, core))

    group = lax.broadcasted_iota(jnp.int32, hot.shape, 0) // 8
    lane = lax.broadcasted_iota(jnp.int32, hot.shape, 1)
    hot[...] = jnp.where(group == lane, 1.0, 0.0).astype(BF16)

    def make_bias(t):
        starts = jnp.broadcast_to(meta[t, 2 * CHUNKS:2 * CHUNKS + 1, :], (block, block)).T
        key_off = lax.broadcasted_iota(jnp.int32, (block, block), 1)
        query_pos = (chip * 2 + t) * block + lax.broadcasted_iota(jnp.int32, (block, block), 0)
        for i in range(CHUNKS):
            for which in (0, 1):
                key_pos = ((chip - backs[i]) * 2 + which) * block + key_off
                line = i * 2 + which
                flags = meta[t, line:line + 1, :]
                seen = (flags == 1) & (key_pos >= starts) & (key_pos <= query_pos)
                bias[t, i, :, which * block:(which + 1) * block] = (
                    jnp.where(seen, 0.0, MASKED).astype(BF16))

    def regroup(t):
        def piece(i, _):
            at = pl.ds(pl.multiple_of(i * 64, 64), 64)
            raw = qraw[t, at].astype(F32)
            to = pl.ds(pl.multiple_of(i * 512, 512), 512)
            qbuf[t, 0, to, :] = raw[:, :8, :].reshape(512, 128).astype(BF16)
            qbuf[t, 1, to, :] = raw[:, 8:, :].reshape(512, 128).astype(BF16)
            return 0
        lax.fori_loop(0, block // 64, piece, 0)

    scale = 1.0 / math.sqrt(128)
    ones = jnp.ones((2 * block, 128), BF16)
    tiles = block * 8 // TILE

    def run(stage, t):
        first, last = stage == 0, stage == len(STAGES) - 1
        units = [(r, h) for r in range(tiles) for h in (0, 1)]

        def score(r, h):
            at = slice(r * TILE, (r + 1) * TILE)
            lhs = jnp.concatenate([qbuf[t, h, at, :], hot[at, :]], axis=1)
            parts = []
            for i in STAGES[stage]:
                keys = jnp.concatenate([kvbuf[slots[i], 0, 0, h], kvbuf[slots[i], 1, 0, h]], axis=1)
                keys = jnp.concatenate([keys, bias[t, i]], axis=0)
                parts.append(jnp.dot(lhs, keys, preferred_element_type=F32))
            return parts

        done = []
        ready = score(*units[0])
        for n, (r, h) in enumerate(units):
            at = slice(r * TILE, (r + 1) * TILE)
            parts = ready
            if n + 1 < len(units):
                ready = score(*units[n + 1])
            high = functools.reduce(jnp.maximum, parts)
            new_top = jnp.broadcast_to(jnp.max(high, axis=1, keepdims=True), (TILE, 128))
            if not first:
                old_top = top[t, h, at, :]
                new_top = jnp.maximum(old_top, new_top)
            wide_top = jnp.concatenate([new_top, new_top], axis=1)
            total = None
            for i, part in zip(STAGES[stage], parts):
                weights = jnp.exp((part - wide_top) * scale).astype(BF16)
                values = jnp.concatenate([kvbuf[slots[i], 0, 1, h], kvbuf[slots[i], 1, 1, h]], axis=0)
                values = jnp.concatenate([values, ones], axis=1)
                product = jnp.dot(weights, values, preferred_element_type=F32)
                total = product if total is None else total + product
            if not first:
                factor = jnp.exp((old_top - new_top) * scale)
                total = total + acc[t, h, at, :] * jnp.concatenate([factor, factor], axis=1)
            if last:
                done.append((total[:, :128] / total[:, 128:]).reshape(TILE // 8, 8, 128))
                if h == 1:
                    both = jnp.concatenate(done[-2:], axis=1).astype(BF16)
                    ostage[t, r * (TILE // 8):(r + 1) * (TILE // 8)] = both
            else:
                acc[t, h, at, :] = total
                top[t, h, at, :] = new_top

    def run_both(stage):
        def step(t, _):
            run(stage, t)
            return 0
        lax.fori_loop(0, 2, step, 0)

    make_bias(core)
    own_q.wait()
    regroup(core)
    own_kv.wait()
    arrived(kvbuf.at[0, other], mate_recv.at[2])
    for i, offset in enumerate(OFFSETS):
        @pl.when(y + offset < ring)
        def _():
            along(i, offset, 0).start()
    arrived(meta.at[other], mate_recv.at[0])
    arrived(qraw.at[other], mate_recv.at[1])
    make_bias(other)
    regroup(other)
    run_both(0)
    for slot in (2, 1, 3):
        for which in (0, 1):
            arrived(kvbuf.at[slot, which], one_recv.at[slot - 1, which])
    for i, offset in enumerate(OFFSETS):
        @pl.when(y + offset >= ring)
        def _():
            along(i, offset, 0).start()
        along(i, offset, 1).start()
    run_both(1)
    for stage in range(2, 5):
        for cross in (0, 1):
            arrived(kvbuf.at[2 * stage + cross], two_recv.at[stage - 2, cross])
        if stage < 4:
            run_both(stage)

    def finish(t, _):
        t = jnp.where(t == 0, other, core)
        run(4, t)

        @pl.when(t == other)
        def _():
            remote(ostage.at[other], out_hbm.at[:, half(core), :],
                   mate_send.at[3], mate_recv.at[3], mate).start()
        return 0

    lax.fori_loop(0, 2, finish, 0)
    own_out = pltpu.make_async_copy(ostage.at[core], out_hbm.at[:, half(core), :], here.at[0])
    own_out.start()
    for send in sends:
        send.wait_send()
    for i, offset in enumerate(OFFSETS):
        for cross in (0, 1):
            along(i, offset, cross).wait_send()
    own_out.wait()
    remote(ostage.at[other], out_hbm.at[:, half(core), :],
           mate_send.at[3], mate_recv.at[3], mate).wait_send()
    arrived(out_hbm.at[:, half(other), :], mate_recv.at[3])


def local(queries, rotated_key_rows, value_matrix_rows, doc_start, block_keep):
    block = queries.shape[0]
    rows, cols = lax.axis_size("row"), lax.axis_size("col")
    kv = jnp.stack([rotated_key_rows, value_matrix_rows])
    kv = kv.reshape(2, block, 2, 2, 128).transpose(2, 0, 3, 1, 4)
    vmem = pl.BlockSpec(memory_space=pltpu.VMEM)
    hbm = pl.BlockSpec(memory_space=pl.ANY)
    return pl.pallas_call(
        functools.partial(kernel, rows, cols),
        out_shape=jax.ShapeDtypeStruct(queries.shape, BF16),
        in_specs=[hbm, vmem, vmem, pl.BlockSpec(memory_space=pltpu.SMEM)],
        out_specs=hbm,
        scratch_shapes=[
            pltpu.VMEM((10, 2, 2, 2, block, 128), BF16),
            pltpu.VMEM((2, 2, 2, block, 128), BF16),
            pltpu.VMEM((2, block, 16, 128), BF16),
            pltpu.VMEM((2, 24, 128), jnp.int32),
            pltpu.VMEM((2, 2, block * 8, 128), BF16),
            pltpu.VMEM((block * 8, 128), BF16),
            pltpu.VMEM((2, CHUNKS, block, 2 * block), BF16),
            pltpu.VMEM((2, 2, block * 8, 256), F32),
            pltpu.VMEM((2, 2, block * 8, 128), F32),
            pltpu.VMEM((2, block, 16, 128), BF16),
            pltpu.SemaphoreType.DMA((3, 2)),
            pltpu.SemaphoreType.DMA((3, 2)),
            pltpu.SemaphoreType.DMA((3, 2)),
            pltpu.SemaphoreType.DMA((3, 2)),
            pltpu.SemaphoreType.DMA((4,)),
            pltpu.SemaphoreType.DMA((4,)),
            pltpu.SemaphoreType.DMA((2,)),
        ],
        compiler_params=pltpu.CompilerParams(
            collective_id=0, has_side_effects=True, vmem_limit_bytes=48 * 1024 * 1024),
        cost_estimate=pl.CostEstimate(flops=10**10, bytes_accessed=8 * 10**6, transcendentals=10**7),
    )(queries, kv, doc_start.reshape(1, block), block_keep)


def solution(mesh):
    return jax.shard_map(
        local,
        mesh=mesh,
        in_specs=(
            P(("col", "row"), None, None),
            P(("col", "row"), None, None),
            P(("col", "row"), None, None),
            P(("col", "row")),
            P(("col", "row"), None),
        ),
        out_specs=P(("col", "row"), None, None),
        check_vma=False,
    )
```

```python
import functools
import math

import jax
import jax.numpy as jnp
from jax import lax
from jax.experimental import pallas as pl
from jax.experimental.pallas import tpu as pltpu
from jax.sharding import PartitionSpec as P

MASKED = -1e30
STAGES = ((0,), (1, 2), (3, 4), (5, 6), (7, 8))
OFFSETS = (1, 3, 2)
X_TRANSIT, Y_TRANSIT = 10, 11
CHUNKS = 9
TILE = 512
F32, BF16 = jnp.float32, jnp.bfloat16


def kernel(rows, cols, q_hbm, kv_ref, start_ref, keep_ref, out_hbm,
           kvbuf, kvs, qraw, meta, qbuf, hot, bias, acc, top, ostage,
           one_send, one_recv, two_send, two_recv, pass_send, pass_recv,
           mate_send, mate_recv, here):
    block = q_hbm.shape[0]
    per_seg = rows // 2
    ring = per_seg // 2
    row, col = lax.axis_index("row"), lax.axis_index("col")
    core = lax.rem(row, 2)
    other = 1 - core
    place = row // 2
    side = lax.rem(place, 2)
    y = place // 2
    chip = col * per_seg + place
    next_col = lax.rem(col + 1, cols)
    last_col = lax.rem(col + cols - 1, cols)

    def device(seg, at_y, at_side, which):
        return {"row": (at_y * 2 + at_side) * 2 + which, "col": seg}

    mate = device(col, y, side, other)

    def beside(step, which):
        x = lax.rem(side * 2 + lax.rem(col, 2) + step + 4, 4)
        return device(col - lax.rem(col, 2) + lax.rem(x, 2), y, x // 2, which)

    def above(step):
        return device(col, lax.rem(y + step + ring, ring), side, core)

    way = 1 - 2 * core

    def remote(src, dst, send, recv, target):
        return pltpu.make_async_remote_copy(
            src_ref=src, dst_ref=dst, send_sem=send, recv_sem=recv,
            device_id=target, device_id_type=pl.DeviceIdType.MESH)

    def arrived(dst, sem):
        remote(dst, dst, mate_send.at[0], sem, mate).wait_recv()

    barrier = pltpu.get_barrier_semaphore()

    def greet(target):
        pl.semaphore_signal(barrier, inc=1, device_id=target, device_id_type=pl.DeviceIdType.MESH)

    greet(mate)
    for which in (0, 1):
        greet(beside(-way, which))

    @pl.when(col > 0)
    def _():
        for which in (0, 1):
            greet(device(last_col, y, side, which))
            greet(device(last_col, y, 1 - side, which))

    @pl.when(col == 0)
    def _():
        kvbuf[2:4] = jnp.zeros((2,) + kvbuf.shape[1:], BF16)

    greet(above(1))
    greet(above(-1))

    def half(which):
        return pl.ds(pl.multiple_of(which * 16, 16), 16)

    own_q = pltpu.make_async_copy(q_hbm.at[:, half(core), :], qraw.at[core], here.at[0])
    own_q.start()

    for which in (0, 1):
        for h in (0, 1):
            kvs[which, 0, h] = kv_ref[which, 0, h]
            kvs[which, 1, h] = kv_ref[which, 1, h].astype(F32).T.astype(BF16)
    own_kv = pltpu.make_async_copy(kvs.at[core], kvbuf.at[0, core], here.at[1])
    own_kv.start()

    backs = [0, 7 - 6 * side, 8]
    slots = [0, 3 - 2 * side, 2]
    for place_at, offset in enumerate(OFFSETS):
        backs += [2 * offset, 2 * offset - 1 + 2 * side]
        slots += [4 + 2 * place_at, 5 + 2 * place_at]

    own_block = chip * 2 + core
    for i in range(CHUNKS):
        for which in (0, 1):
            number = (chip - backs[i]) * 2 + which
            flag = keep_ref[0, jnp.maximum(number, 0)]
            flag = jnp.where(number == own_block, 1, flag)
            line = i * 2 + which
            meta[core, line:line + 1, :] = jnp.full((1, block), flag, jnp.int32)
    line = 2 * CHUNKS
    meta[core, line:line + 1, :] = start_ref[...]

    pl.semaphore_wait(barrier, jnp.where(col < cols - 1, 9, 5))

    sends = [
        remote(kvs.at[other], kvbuf.at[0, core], mate_send.at[2], mate_recv.at[2], mate),
        remote(meta.at[core], meta.at[core], mate_send.at[0], mate_recv.at[0], mate),
        remote(q_hbm.at[:, half(other), :], qraw.at[core], mate_send.at[1], mate_recv.at[1], mate),
    ]
    for which in (0, 1):
        sends.append(remote(kvs.at[which], kvbuf.at[X_TRANSIT, core],
                            one_send.at[0, which], one_recv.at[0, core],
                            beside(1 - 2 * which, which)))
    onward = []
    for slot, at_side in ((2, side), (3, 1 - side)):
        for which in (0, 1):
            onward.append(remote(kvs.at[which], kvbuf.at[slot, core],
                                 one_send.at[slot - 1, which], one_recv.at[slot - 1, core],
                                 device(next_col, y, at_side, which)))
    for send in sends:
        send.start()

    @pl.when(col < cols - 1)
    def _():
        for send in onward:
            send.start()

    def along(i, cross):
        offset = OFFSETS[i]
        held = y + offset < ring
        source = jnp.where(held, 0, 2) + cross
        to = (Y_TRANSIT if offset == 2 else 4 + 2 * i) + cross
        target = above(way) if offset == 2 else above(1 if offset == 1 else -1)
        return remote(kvbuf.at[source], kvbuf.at[to], two_send.at[i, cross], two_recv.at[i, cross],
                      target)

    pass_x = remote(kvbuf.at[X_TRANSIT], kvbuf.at[1], pass_send.at[0], pass_recv.at[0],
                    beside(way, core))
    pass_y = [remote(kvbuf.at[Y_TRANSIT + cross], kvbuf.at[8 + cross],
                     pass_send.at[1 + cross], pass_recv.at[1 + cross], above(way))
              for cross in (0, 1)]

    group = lax.broadcasted_iota(jnp.int32, hot.shape, 1) // 8
    token = lax.broadcasted_iota(jnp.int32, hot.shape, 0)
    hot[...] = jnp.where(group == token, 1.0, 0.0).astype(BF16)

    def make_bias(t):
        starts = meta[t, 2 * CHUNKS:2 * CHUNKS + 1, :]
        key_off = lax.broadcasted_iota(jnp.int32, (block, block), 0)
        query_pos = (chip * 2 + t) * block + lax.broadcasted_iota(jnp.int32, (block, block), 1)
        for i in range(CHUNKS):
            for which in (0, 1):
                key_pos = ((chip - backs[i]) * 2 + which) * block + key_off
                line = i * 2 + which
                flags = meta[t, line:line + 1, :]
                seen = (flags == 1) & (key_pos >= starts) & (key_pos <= query_pos)
                bias[t, i, which * block:(which + 1) * block, :] = (
                    jnp.where(seen, 0.0, MASKED).astype(BF16))

    def regroup(t):
        def piece(i, _):
            at = pl.ds(pl.multiple_of(i * 64, 64), 64)
            raw = qraw[t, at].astype(F32)
            to = pl.ds(pl.multiple_of(i * 512, 512), 512)
            qbuf[t, 0, :, to] = raw[:, :8, :].reshape(512, 128).T.astype(BF16)
            qbuf[t, 1, :, to] = raw[:, 8:, :].reshape(512, 128).T.astype(BF16)
            return 0
        lax.fori_loop(0, block // 64, piece, 0)

    scale = 1.0 / math.sqrt(128)
    tiles = block * 8 // TILE

    def run(stage, t):
        first, last = stage == 0, stage == len(STAGES) - 1
        used = STAGES[stage]
        ones = jnp.ones((16, len(used) * 2 * block), BF16)
        units = [(r, h) for r in range(tiles) for h in (0, 1)]

        def score(r, h):
            at = slice(r * TILE, (r + 1) * TILE)
            rhs = jnp.concatenate([qbuf[t, h, :, at], hot[:, at]], axis=0)
            keys = jnp.concatenate(
                [kvbuf[slots[i], which, 0, h] for i in used for which in (0, 1)], axis=0)
            masks = jnp.concatenate([bias[t, i] for i in used], axis=0)
            return jnp.dot(jnp.concatenate([keys, masks], axis=1), rhs, preferred_element_type=F32)

        done = []
        ready = score(*units[0])
        for n, (r, h) in enumerate(units):
            at = slice(r * TILE, (r + 1) * TILE)
            scores = ready
            if n + 1 < len(units):
                ready = score(*units[n + 1])
            new_top = jnp.max(scores, axis=0, keepdims=True)
            if not first:
                old_top = top[t, h, 0:1, at]
                new_top = jnp.maximum(old_top, new_top)
            weights = jnp.exp((scores - new_top) * scale).astype(BF16)
            values = jnp.concatenate(
                [kvbuf[slots[i], which, 1, h] for i in used for which in (0, 1)], axis=1)
            total = jnp.dot(jnp.concatenate([values, ones], axis=0), weights,
                            preferred_element_type=F32)
            if not first:
                total = total + acc[t, h, :, at] * jnp.exp((old_top - new_top) * scale)
            if last:
                result = total[:128] / total[128:129]
                done.append(result.T.reshape(TILE // 8, 8, 128))
                if h == 1:
                    both = jnp.concatenate(done[-2:], axis=1).astype(BF16)
                    ostage[t, r * (TILE // 8):(r + 1) * (TILE // 8)] = both
            else:
                acc[t, h, :, at] = total
                top[t, h, 0:1, at] = new_top

    def run_both(stage, between=None):
        def step(t, _):
            run(stage, t)
            if between is not None:
                @pl.when(t == 0)
                def _():
                    between()
            return 0
        lax.fori_loop(0, 2, step, 0)

    def start_own(early):
        for i in (2, 0, 1):
            held = y + OFFSETS[i] < ring

            @pl.when(held if early else jnp.logical_not(held))
            def _():
                along(i, 0).start()

    def hand_on(cross):
        arrived(kvbuf.at[Y_TRANSIT + cross], two_recv.at[2, cross])
        pass_y[cross].start()

    def before(slot):
        @pl.when(col > 0)
        def _():
            for which in (0, 1):
                arrived(kvbuf.at[slot, which], one_recv.at[slot - 1, which])

    def previous():
        before(2)
        start_own(False)

    make_bias(core)
    own_q.wait()
    regroup(core)
    own_kv.wait()
    arrived(kvbuf.at[0, other], mate_recv.at[2])
    start_own(True)
    arrived(meta.at[other], mate_recv.at[0])
    arrived(qraw.at[other], mate_recv.at[1])
    make_bias(other)
    regroup(other)
    for which in (0, 1):
        arrived(kvbuf.at[X_TRANSIT, which], one_recv.at[0, which])
    pass_x.start()
    run_both(0, previous)
    arrived(kvbuf.at[1], pass_recv.at[0])
    before(3)
    for i in (2, 0, 1):
        along(i, 1).start()
    run_both(1, lambda: hand_on(0))
    hand_on(1)
    for stage in (2, 3):
        for cross in (0, 1):
            arrived(kvbuf.at[2 * stage + cross], two_recv.at[stage - 2, cross])
        run_both(stage)
    for cross in (0, 1):
        arrived(kvbuf.at[8 + cross], pass_recv.at[1 + cross])

    def finish(t, _):
        t = jnp.where(t == 0, other, core)
        run(4, t)

        @pl.when(t == other)
        def _():
            remote(ostage.at[other], out_hbm.at[:, half(core), :],
                   mate_send.at[3], mate_recv.at[3], mate).start()
        return 0

    lax.fori_loop(0, 2, finish, 0)
    own_out = pltpu.make_async_copy(ostage.at[core], out_hbm.at[:, half(core), :], here.at[0])
    own_out.start()
    for send in sends:
        send.wait_send()

    @pl.when(col < cols - 1)
    def _():
        for send in onward:
            send.wait_send()

    for i in range(3):
        for cross in (0, 1):
            along(i, cross).wait_send()
    pass_x.wait_send()
    for copy in pass_y:
        copy.wait_send()
    own_out.wait()
    remote(ostage.at[other], out_hbm.at[:, half(core), :],
           mate_send.at[3], mate_recv.at[3], mate).wait_send()
    arrived(out_hbm.at[:, half(other), :], mate_recv.at[3])


def local(queries, rotated_key_rows, value_matrix_rows, doc_start, block_keep):
    block = queries.shape[0]
    rows, cols = lax.axis_size("row"), lax.axis_size("col")
    kv = jnp.stack([rotated_key_rows, value_matrix_rows])
    kv = kv.reshape(2, block, 2, 2, 128).transpose(2, 0, 3, 1, 4)
    vmem = pl.BlockSpec(memory_space=pltpu.VMEM)
    hbm = pl.BlockSpec(memory_space=pl.ANY)
    return pl.pallas_call(
        functools.partial(kernel, rows, cols),
        out_shape=jax.ShapeDtypeStruct(queries.shape, BF16),
        in_specs=[hbm, vmem, vmem, pl.BlockSpec(memory_space=pltpu.SMEM)],
        out_specs=hbm,
        scratch_shapes=[
            pltpu.VMEM((13, 2, 2, 2, block, 128), BF16),
            pltpu.VMEM((2, 2, 2, block, 128), BF16),
            pltpu.VMEM((2, block, 16, 128), BF16),
            pltpu.VMEM((2, 24, 128), jnp.int32),
            pltpu.VMEM((2, 2, 128, block * 8), BF16),
            pltpu.VMEM((block, block * 8), BF16),
            pltpu.VMEM((2, CHUNKS, 2 * block, block), BF16),
            pltpu.VMEM((2, 2, 144, block * 8), F32),
            pltpu.VMEM((2, 2, 8, block * 8), F32),
            pltpu.VMEM((2, block, 16, 128), BF16),
            pltpu.SemaphoreType.DMA((3, 2)),
            pltpu.SemaphoreType.DMA((3, 2)),
            pltpu.SemaphoreType.DMA((3, 2)),
            pltpu.SemaphoreType.DMA((3, 2)),
            pltpu.SemaphoreType.DMA((3,)),
            pltpu.SemaphoreType.DMA((3,)),
            pltpu.SemaphoreType.DMA((4,)),
            pltpu.SemaphoreType.DMA((4,)),
            pltpu.SemaphoreType.DMA((2,)),
        ],
        compiler_params=pltpu.CompilerParams(
            collective_id=0, has_side_effects=True, vmem_limit_bytes=48 * 1024 * 1024),
        cost_estimate=pl.CostEstimate(flops=10**10, bytes_accessed=8 * 10**6, transcendentals=10**7),
    )(queries, kv, doc_start.reshape(1, block), block_keep)


def solution(mesh):
    return jax.shard_map(
        local,
        mesh=mesh,
        in_specs=(
            P(("col", "row"), None, None),
            P(("col", "row"), None, None),
            P(("col", "row"), None, None),
            P(("col", "row")),
            P(("col", "row"), None),
        ),
        out_specs=P(("col", "row"), None, None),
        check_vma=False,
    )
```

```python
import functools
import math

import jax
import jax.numpy as jnp
from jax import lax
from jax.experimental import pallas as pl
from jax.experimental.pallas import tpu as pltpu
from jax.sharding import PartitionSpec as P

MASKED = -1e30
STAGES = ((0,), (1, 2), (3, 5), (7, 4), (6, 8))
OFFSETS = (1, 3, 2)
X_TRANSIT, Y_TRANSIT, LATE_TRANSIT = 10, 11, 12
CHUNKS = 9
TILE = 512
F32, BF16 = jnp.float32, jnp.bfloat16


def kernel(rows, cols, q_hbm, k_hbm, v_hbm, start_ref, keep_ref, out_hbm,
           kvbuf, kvs, kvraw, qraw, meta, qbuf, hot, bias, acc, top, ostage,
           one_send, one_recv, two_send, two_recv, pass_send, pass_recv,
           mate_send, mate_recv, here):
    block = q_hbm.shape[0]
    per_seg = rows // 2
    ring = per_seg // 2
    row, col = lax.axis_index("row"), lax.axis_index("col")
    core = lax.rem(row, 2)
    other = 1 - core
    place = row // 2
    side = lax.rem(place, 2)
    y = place // 2
    chip = col * per_seg + place
    next_col = lax.rem(col + 1, cols)
    last_col = lax.rem(col + cols - 1, cols)

    def device(seg, at_y, at_side, which):
        return {"row": (at_y * 2 + at_side) * 2 + which, "col": seg}

    mate = device(col, y, side, other)

    def beside(step, which):
        x = lax.rem(side * 2 + lax.rem(col, 2) + step + 4, 4)
        return device(col - lax.rem(col, 2) + lax.rem(x, 2), y, x // 2, which)

    def above(step):
        return device(col, lax.rem(y + step + ring, ring), side, core)

    way = 1 - 2 * core

    def remote(src, dst, send, recv, target):
        return pltpu.make_async_remote_copy(
            src_ref=src, dst_ref=dst, send_sem=send, recv_sem=recv,
            device_id=target, device_id_type=pl.DeviceIdType.MESH)

    def arrived(dst, sem):
        remote(dst, dst, mate_send.at[0], sem, mate).wait_recv()

    own_raw = [pltpu.make_async_copy(k_hbm, kvraw.at[0], here.at[1]),
               pltpu.make_async_copy(v_hbm, kvraw.at[1], here.at[2])]
    for copy in own_raw:
        copy.start()
    barrier = pltpu.get_barrier_semaphore()

    def greet(target):
        pl.semaphore_signal(barrier, inc=1, device_id=target, device_id_type=pl.DeviceIdType.MESH)

    greet(mate)
    for which in (0, 1):
        greet(beside(-way, which))

    @pl.when(col > 0)
    def _():
        for which in (0, 1):
            greet(device(last_col, y, side, which))
            greet(device(last_col, y, 1 - side, which))

    @pl.when(col == 0)
    def _():
        kvbuf[2:4] = jnp.zeros((2,) + kvbuf.shape[1:], BF16)

    greet(above(1))
    greet(above(-1))

    def half(which):
        return pl.ds(pl.multiple_of(which * 16, 16), 16)

    own_q = pltpu.make_async_copy(q_hbm.at[:, half(core), :], qraw.at[core], here.at[0])
    own_q.start()

    for copy in own_raw:
        copy.wait()
    all_keys, all_values = kvraw[0].astype(F32), kvraw[1].astype(F32)
    for which in (0, 1):
        for h in (0, 1):
            kvs[which, 0, h] = all_keys[:, 2 * which + h, :].astype(BF16)
            kvs[which, 1, h] = all_values[:, 2 * which + h, :].T.astype(BF16)
    own_kv = pltpu.make_async_copy(kvs.at[core], kvbuf.at[0, core], here.at[1])
    own_kv.start()

    backs = [0, 7 - 6 * side, 8]
    slots = [0, 3 - 2 * side, 2]
    for place_at, offset in enumerate(OFFSETS):
        backs += [2 * offset, 2 * offset - 1 + 2 * side]
        slots += [4 + 2 * place_at, 5 + 2 * place_at]

    own_block = chip * 2 + core
    for i in range(CHUNKS):
        for which in (0, 1):
            number = (chip - backs[i]) * 2 + which
            flag = keep_ref[0, jnp.maximum(number, 0)]
            flag = jnp.where(number == own_block, 1, flag)
            line = i * 2 + which
            meta[core, line:line + 1, :] = jnp.full((1, block), flag, jnp.int32)
    line = 2 * CHUNKS
    meta[core, line:line + 1, :] = start_ref[...]

    pl.semaphore_wait(barrier, jnp.where(col < cols - 1, 9, 5))

    sends = [
        remote(kvs.at[other], kvbuf.at[0, core], mate_send.at[2], mate_recv.at[2], mate),
        remote(meta.at[core], meta.at[core], mate_send.at[0], mate_recv.at[0], mate),
        remote(q_hbm.at[:, half(other), :], qraw.at[core], mate_send.at[1], mate_recv.at[1], mate),
    ]
    for which in (0, 1):
        sends.append(remote(kvs.at[which], kvbuf.at[X_TRANSIT, core],
                            one_send.at[0, which], one_recv.at[0, core],
                            beside(1 - 2 * which, which)))
    onward = []
    for slot, at_side in ((2, side), (3, 1 - side)):
        for which in (0, 1):
            onward.append(remote(kvs.at[which], kvbuf.at[slot, core],
                                 one_send.at[slot - 1, which], one_recv.at[slot - 1, core],
                                 device(next_col, y, at_side, which)))
    for send in sends:
        send.start()

    @pl.when(col < cols - 1)
    def _():
        for send in onward:
            send.start()

    def along(i, cross):
        offset = OFFSETS[i]
        held = y + offset < ring
        source = jnp.where(held, 0, 2) + cross
        to = (Y_TRANSIT if offset == 2 else 4 + 2 * i) + cross
        target = above(way) if offset == 2 else above(1 if offset == 1 else -1)
        return remote(kvbuf.at[source], kvbuf.at[to], two_send.at[i, cross], two_recv.at[i, cross],
                      target)

    pass_x = remote(kvbuf.at[X_TRANSIT], kvbuf.at[1], pass_send.at[0], pass_recv.at[0],
                    beside(way, core))
    pass_y = remote(kvbuf.at[Y_TRANSIT], kvbuf.at[8], pass_send.at[1], pass_recv.at[1], above(way))
    late = remote(kvbuf.at[8], kvbuf.at[LATE_TRANSIT], two_send.at[2, 1], two_recv.at[2, 1],
                  beside(way, core))
    pass_late = remote(kvbuf.at[LATE_TRANSIT], kvbuf.at[9], pass_send.at[2], pass_recv.at[2],
                       beside(way, core))

    group = lax.broadcasted_iota(jnp.int32, hot.shape, 1) // 8
    token = lax.broadcasted_iota(jnp.int32, hot.shape, 0)
    hot[...] = jnp.where(group == token, 1.0, 0.0).astype(BF16)

    def make_bias(t):
        starts = meta[t, 2 * CHUNKS:2 * CHUNKS + 1, :]
        key_off = lax.broadcasted_iota(jnp.int32, (block, block), 0)
        query_pos = (chip * 2 + t) * block + lax.broadcasted_iota(jnp.int32, (block, block), 1)
        for i in range(CHUNKS):
            for which in (0, 1):
                key_pos = ((chip - backs[i]) * 2 + which) * block + key_off
                line = i * 2 + which
                flags = meta[t, line:line + 1, :]
                seen = (flags == 1) & (key_pos >= starts) & (key_pos <= query_pos)
                bias[t, i, which * block:(which + 1) * block, :] = (
                    jnp.where(seen, 0.0, MASKED).astype(BF16))

    def regroup(t):
        def piece(i, _):
            at = pl.ds(pl.multiple_of(i * 64, 64), 64)
            raw = qraw[t, at].astype(F32)
            to = pl.ds(pl.multiple_of(i * 512, 512), 512)
            qbuf[t, 0, :, to] = raw[:, :8, :].reshape(512, 128).T.astype(BF16)
            qbuf[t, 1, :, to] = raw[:, 8:, :].reshape(512, 128).T.astype(BF16)
            return 0
        lax.fori_loop(0, block // 64, piece, 0)

    scale = 1.0 / math.sqrt(128)
    tiles = block * 8 // TILE

    def run(stage, t):
        first, last = stage == 0, stage == len(STAGES) - 1
        used = STAGES[stage]
        ones = jnp.ones((16, len(used) * 2 * block), BF16)
        units = [(r, h) for r in range(tiles) for h in (0, 1)]

        def score(r, h):
            at = slice(r * TILE, (r + 1) * TILE)
            rhs = jnp.concatenate([qbuf[t, h, :, at], hot[:, at]], axis=0)
            keys = jnp.concatenate(
                [kvbuf[slots[i], which, 0, h] for i in used for which in (0, 1)], axis=0)
            masks = jnp.concatenate([bias[t, i] for i in used], axis=0)
            return jnp.dot(jnp.concatenate([keys, masks], axis=1), rhs, preferred_element_type=F32)

        done = []
        ready = score(*units[0])
        for n, (r, h) in enumerate(units):
            at = slice(r * TILE, (r + 1) * TILE)
            scores = ready
            if n + 1 < len(units):
                ready = score(*units[n + 1])
            new_top = jnp.max(scores, axis=0, keepdims=True)
            if not first:
                old_top = top[t, h, 0:1, at]
                new_top = jnp.maximum(old_top, new_top)
            weights = jnp.exp((scores - new_top) * scale).astype(BF16)
            values = jnp.concatenate(
                [kvbuf[slots[i], which, 1, h] for i in used for which in (0, 1)], axis=1)
            total = jnp.dot(jnp.concatenate([values, ones], axis=0), weights,
                            preferred_element_type=F32)
            if not first:
                total = total + acc[t, h, :, at] * jnp.exp((old_top - new_top) * scale)
            if last:
                result = total[:128] / total[128:129]
                done.append(result.T.reshape(TILE // 8, 8, 128))
                if h == 1:
                    both = jnp.concatenate(done[-2:], axis=1).astype(BF16)
                    ostage[t, r * (TILE // 8):(r + 1) * (TILE // 8)] = both
            else:
                acc[t, h, :, at] = total
                top[t, h, 0:1, at] = new_top

    def run_both(stage, between=None):
        def step(t, _):
            run(stage, t)
            if between is not None:
                @pl.when(t == 0)
                def _():
                    between()
            return 0
        lax.fori_loop(0, 2, step, 0)

    def start_own(early):
        for i in (2, 0, 1):
            held = y + OFFSETS[i] < ring

            @pl.when(held if early else jnp.logical_not(held))
            def _():
                along(i, 0).start()

    def far():
        arrived(kvbuf.at[Y_TRANSIT], two_recv.at[2, 0])
        pass_y.start()

    def far_here():
        arrived(kvbuf.at[8], pass_recv.at[1])
        late.start()

    def far_on():
        arrived(kvbuf.at[LATE_TRANSIT], two_recv.at[2, 1])
        pass_late.start()

    def before(slot):
        @pl.when(col > 0)
        def _():
            for which in (0, 1):
                arrived(kvbuf.at[slot, which], one_recv.at[slot - 1, which])

    def previous():
        before(2)
        start_own(False)

    make_bias(core)
    own_q.wait()
    regroup(core)
    own_kv.wait()
    arrived(kvbuf.at[0, other], mate_recv.at[2])
    start_own(True)
    arrived(meta.at[other], mate_recv.at[0])
    arrived(qraw.at[other], mate_recv.at[1])
    make_bias(other)
    regroup(other)
    for which in (0, 1):
        arrived(kvbuf.at[X_TRANSIT, which], one_recv.at[0, which])
    pass_x.start()
    run_both(0, previous)
    arrived(kvbuf.at[1], pass_recv.at[0])
    before(3)
    for i in (0, 1):
        along(i, 1).start()
    run_both(1, far)
    for i in (0, 1):
        arrived(kvbuf.at[4 + 2 * i], two_recv.at[i, 0])
    run_both(2, far_here)
    arrived(kvbuf.at[5], two_recv.at[0, 1])
    run_both(3, far_on)
    arrived(kvbuf.at[7], two_recv.at[1, 1])
    arrived(kvbuf.at[9], pass_recv.at[2])

    def finish(t, _):
        t = jnp.where(t == 0, other, core)
        run(4, t)

        @pl.when(t == other)
        def _():
            remote(ostage.at[other], out_hbm.at[:, half(core), :],
                   mate_send.at[3], mate_recv.at[3], mate).start()
        return 0

    lax.fori_loop(0, 2, finish, 0)
    own_out = pltpu.make_async_copy(ostage.at[core], out_hbm.at[:, half(core), :], here.at[0])
    own_out.start()
    for send in sends:
        send.wait_send()

    @pl.when(col < cols - 1)
    def _():
        for send in onward:
            send.wait_send()

    for i in range(3):
        along(i, 0).wait_send()
        if i < 2:
            along(i, 1).wait_send()
    for copy in (pass_x, pass_y, late, pass_late):
        copy.wait_send()
    own_out.wait()
    remote(ostage.at[other], out_hbm.at[:, half(core), :],
           mate_send.at[3], mate_recv.at[3], mate).wait_send()
    arrived(out_hbm.at[:, half(other), :], mate_recv.at[3])


def local(queries, rotated_key_rows, value_matrix_rows, doc_start, block_keep):
    block = queries.shape[0]
    rows, cols = lax.axis_size("row"), lax.axis_size("col")
    vmem = pl.BlockSpec(memory_space=pltpu.VMEM)
    hbm = pl.BlockSpec(memory_space=pl.ANY)
    return pl.pallas_call(
        functools.partial(kernel, rows, cols),
        out_shape=jax.ShapeDtypeStruct(queries.shape, BF16),
        in_specs=[hbm, hbm, hbm, vmem, pl.BlockSpec(memory_space=pltpu.SMEM)],
        out_specs=pl.BlockSpec(memory_space=pl.ANY),
        scratch_shapes=[
            pltpu.VMEM((13, 2, 2, 2, block, 128), BF16),
            pltpu.VMEM((2, 2, 2, block, 128), BF16),
            pltpu.VMEM((2, block, 4, 128), BF16),
            pltpu.VMEM((2, block, 16, 128), BF16),
            pltpu.VMEM((2, 24, 128), jnp.int32),
            pltpu.VMEM((2, 2, 128, block * 8), BF16),
            pltpu.VMEM((block, block * 8), BF16),
            pltpu.VMEM((2, CHUNKS, 2 * block, block), BF16),
            pltpu.VMEM((2, 2, 144, block * 8), F32),
            pltpu.VMEM((2, 2, 8, block * 8), F32),
            pltpu.VMEM((2, block, 16, 128), BF16),
            pltpu.SemaphoreType.DMA((3, 2)),
            pltpu.SemaphoreType.DMA((3, 2)),
            pltpu.SemaphoreType.DMA((3, 2)),
            pltpu.SemaphoreType.DMA((3, 2)),
            pltpu.SemaphoreType.DMA((3,)),
            pltpu.SemaphoreType.DMA((3,)),
            pltpu.SemaphoreType.DMA((4,)),
            pltpu.SemaphoreType.DMA((4,)),
            pltpu.SemaphoreType.DMA((3,)),
        ],
        compiler_params=pltpu.CompilerParams(
            collective_id=0, has_side_effects=True, vmem_limit_bytes=63 * 1024 * 1024),
        cost_estimate=pl.CostEstimate(flops=10**10, bytes_accessed=8 * 10**6, transcendentals=10**7),
    )(queries, rotated_key_rows, value_matrix_rows, doc_start.reshape(1, block), block_keep)


def solution(mesh):
    return jax.shard_map(
        local,
        mesh=mesh,
        in_specs=(
            P(("col", "row"), None, None),
            P(("col", "row"), None, None),
            P(("col", "row"), None, None),
            P(("col", "row")),
            P(("col", "row"), None),
        ),
        out_specs=P(("col", "row"), None, None),
        check_vma=False,
    )
```

```python
import functools
import math

import jax
import jax.numpy as jnp
from jax import lax
from jax.experimental import pallas as pl
from jax.experimental.pallas import tpu as pltpu
from jax.sharding import PartitionSpec as P

MASKED = -1e30
OFFSETS = (1, 3, 2)
X_TRANSIT, Y_TRANSIT = 10, 11
CHUNKS = 9
TILE = 256
TOGETHER = 2
F32, BF16 = jnp.float32, jnp.bfloat16


def kernel(rows, cols, q_hbm, kv_ref, start_ref, keep_ref, out_hbm,
           kvbuf, kvs, qraw, meta, qbuf, hot, bias, acc, top, ostage,
           one_send, one_recv, two_send, two_recv, pass_send, pass_recv,
           mate_send, mate_recv, here):
    block = q_hbm.shape[0]
    per_seg = rows // 2
    ring = per_seg // 2
    row, col = lax.axis_index("row"), lax.axis_index("col")
    core = lax.rem(row, 2)
    other = 1 - core
    place = row // 2
    side = lax.rem(place, 2)
    y = place // 2
    chip = col * per_seg + place
    next_col = lax.rem(col + 1, cols)
    last_col = lax.rem(col + cols - 1, cols)

    def device(seg, at_y, at_side, which):
        return {"row": (at_y * 2 + at_side) * 2 + which, "col": seg}

    mate = device(col, y, side, other)

    def beside(step, which):
        x = lax.rem(side * 2 + lax.rem(col, 2) + step + 4, 4)
        return device(col - lax.rem(col, 2) + lax.rem(x, 2), y, x // 2, which)

    def above(step):
        return device(col, lax.rem(y + step + ring, ring), side, core)

    way = 1 - 2 * core

    def remote(src, dst, send, recv, target):
        return pltpu.make_async_remote_copy(
            src_ref=src, dst_ref=dst, send_sem=send, recv_sem=recv,
            device_id=target, device_id_type=pl.DeviceIdType.MESH)

    def arrived(dst, sem):
        remote(dst, dst, mate_send.at[0], sem, mate).wait_recv()

    barrier = pltpu.get_barrier_semaphore()

    def greet(target):
        pl.semaphore_signal(barrier, inc=1, device_id=target, device_id_type=pl.DeviceIdType.MESH)

    greet(mate)
    for which in (0, 1):
        greet(beside(-way, which))

    @pl.when(col > 0)
    def _():
        for which in (0, 1):
            greet(device(last_col, y, side, which))
            greet(device(last_col, y, 1 - side, which))

    @pl.when(col == 0)
    def _():
        kvbuf[2:4] = jnp.zeros((2,) + kvbuf.shape[1:], BF16)

    greet(above(1))
    greet(above(-1))

    def half(which):
        return pl.ds(pl.multiple_of(which * 16, 16), 16)

    own_q = pltpu.make_async_copy(q_hbm.at[:, half(core), :], qraw.at[core], here.at[0])
    own_q.start()

    for which in (0, 1):
        for h in (0, 1):
            kvs[which, 0, h] = kv_ref[which, 0, h]
            kvs[which, 1, h] = kv_ref[which, 1, h].astype(F32).T.astype(BF16)
    own_kv = pltpu.make_async_copy(kvs.at[core], kvbuf.at[0, core], here.at[1])
    own_kv.start()

    backs = [0, 7 - 6 * side, 8]
    for offset in OFFSETS:
        backs += [2 * offset, 2 * offset - 1 + 2 * side]

    own_block = chip * 2 + core
    for i in range(CHUNKS):
        for which in (0, 1):
            number = (chip - backs[i]) * 2 + which
            flag = keep_ref[0, jnp.maximum(number, 0)]
            flag = jnp.where(number == own_block, 1, flag)
            line = i * 2 + which
            meta[core, line:line + 1, :] = jnp.full((1, block), flag, jnp.int32)
    line = 2 * CHUNKS
    meta[core, line:line + 1, :] = start_ref[...]

    pl.semaphore_wait(barrier, jnp.where(col < cols - 1, 9, 5))

    sends = [
        remote(kvs.at[other], kvbuf.at[0, core], mate_send.at[2], mate_recv.at[2], mate),
        remote(meta.at[core], meta.at[core], mate_send.at[0], mate_recv.at[0], mate),
        remote(q_hbm.at[:, half(other), :], qraw.at[core], mate_send.at[1], mate_recv.at[1], mate),
    ]
    for which in (0, 1):
        sends.append(remote(kvs.at[which], kvbuf.at[X_TRANSIT, core],
                            one_send.at[0, which], one_recv.at[0, core],
                            beside(1 - 2 * which, which)))
    onward = []
    for slot, at_side in ((2, side), (3, 1 - side)):
        for which in (0, 1):
            onward.append(remote(kvs.at[which], kvbuf.at[slot, core],
                                 one_send.at[slot - 1, which], one_recv.at[slot - 1, core],
                                 device(next_col, y, at_side, which)))
    for send in sends:
        send.start()

    @pl.when(col < cols - 1)
    def _():
        for send in onward:
            send.start()

    def along(i, cross):
        offset = OFFSETS[i]
        held = y + offset < ring
        source = jnp.where(held, 0, 2) + cross
        to = (Y_TRANSIT if offset == 2 else 4 + 2 * i) + cross
        target = above(way) if offset == 2 else above(1 if offset == 1 else -1)
        return remote(kvbuf.at[source], kvbuf.at[to], two_send.at[i, cross], two_recv.at[i, cross],
                      target)

    pass_x = remote(kvbuf.at[X_TRANSIT], kvbuf.at[1], pass_send.at[0], pass_recv.at[0],
                    beside(way, core))
    pass_y = [remote(kvbuf.at[Y_TRANSIT + cross], kvbuf.at[8 + cross],
                     pass_send.at[1 + cross], pass_recv.at[1 + cross], above(way))
              for cross in (0, 1)]

    group = lax.broadcasted_iota(jnp.int32, hot.shape, 1) // 8
    token = lax.broadcasted_iota(jnp.int32, hot.shape, 0)
    hot[...] = jnp.where(group == token, 1.0, 0.0).astype(BF16)

    def make_bias(t):
        starts = meta[t, 2 * CHUNKS:2 * CHUNKS + 1, :]
        key_off = lax.broadcasted_iota(jnp.int32, (block, block), 0)
        query_pos = (chip * 2 + t) * block + lax.broadcasted_iota(jnp.int32, (block, block), 1)
        for i in range(CHUNKS):
            for which in (0, 1):
                key_pos = ((chip - backs[i]) * 2 + which) * block + key_off
                line = i * 2 + which
                flags = meta[t, line:line + 1, :]
                seen = (flags == 1) & (key_pos >= starts) & (key_pos <= query_pos)
                bias[t, i, which * block:(which + 1) * block, :] = (
                    jnp.where(seen, 0.0, MASKED).astype(BF16))

    def regroup(t):
        def piece(i, _):
            at = pl.ds(pl.multiple_of(i * 64, 64), 64)
            raw = qraw[t, at].astype(F32)
            to = pl.ds(pl.multiple_of(i * 512, 512), 512)
            qbuf[t, 0, :, to] = raw[:, :8, :].reshape(512, 128).T.astype(BF16)
            qbuf[t, 1, :, to] = raw[:, 8:, :].reshape(512, 128).T.astype(BF16)
            return 0
        lax.fori_loop(0, block // 64, piece, 0)

    scale = 1.0 / math.sqrt(128)
    tiles = block * 8 // TILE

    def run(t, used, places, first):
        ones = jnp.ones((16, len(used) * 2 * block), BF16)

        def step(j, _):
            units = [(pl.ds(pl.multiple_of((j * TOGETHER + r) * TILE, TILE), TILE), h)
                     for r in range(TOGETHER) for h in (0, 1)]

            def score(at, h):
                rhs = jnp.concatenate([qbuf[t, h, :, at], hot[:, at]], axis=0)
                keys = jnp.concatenate(
                    [kvbuf[slot, which, 0, h] for slot in places for which in (0, 1)], axis=0)
                masks = jnp.concatenate([bias[t, i] for i in used], axis=0)
                return jnp.dot(jnp.concatenate([keys, masks], axis=1), rhs,
                               preferred_element_type=F32)

            ready = score(*units[0])
            for n, (at, h) in enumerate(units):
                scores = ready
                if n + 1 < len(units):
                    ready = score(*units[n + 1])
                new_top = jnp.max(scores, axis=0, keepdims=True)
                if not first:
                    old_top = top[t, h, 0:1, at]
                    new_top = jnp.maximum(old_top, new_top)
                weights = jnp.exp((scores - new_top) * scale).astype(BF16)
                values = jnp.concatenate(
                    [kvbuf[slot, which, 1, h] for slot in places for which in (0, 1)], axis=1)
                total = jnp.dot(jnp.concatenate([values, ones], axis=0), weights,
                                preferred_element_type=F32)
                if not first:
                    total = total + acc[t, h, :, at] * jnp.exp((old_top - new_top) * scale)
                acc[t, h, :, at] = total
                top[t, h, 0:1, at] = new_top
            return 0

        lax.fori_loop(0, tiles // TOGETHER, step, 0)

    def finish(t):
        def step(r, _):
            at = pl.ds(pl.multiple_of(r * TILE, TILE), TILE)
            done = []
            for h in (0, 1):
                result = acc[t, h, :128, at] / acc[t, h, 128:129, at]
                done.append(result.T.reshape(TILE // 8, 8, 128))
            to = pl.ds(pl.multiple_of(r * (TILE // 8), TILE // 8), TILE // 8)
            ostage[t, to] = jnp.concatenate(done, axis=1).astype(BF16)
            return 0
        lax.fori_loop(0, tiles, step, 0)

    def start_own(early):
        for i in (2, 0, 1):
            held = y + OFFSETS[i] < ring

            @pl.when(held if early else jnp.logical_not(held))
            def _():
                along(i, 0).start()

    def hand_on(cross):
        arrived(kvbuf.at[Y_TRANSIT + cross], two_recv.at[2, cross])
        pass_y[cross].start()

    def before(slot):
        @pl.when(col > 0)
        def _():
            for which in (0, 1):
                arrived(kvbuf.at[slot, which], one_recv.at[slot - 1, which])

    def previous():
        before(2)
        start_own(False)

    make_bias(core)
    own_q.wait()
    regroup(core)
    own_kv.wait()
    arrived(kvbuf.at[0, other], mate_recv.at[2])
    start_own(True)
    arrived(meta.at[other], mate_recv.at[0])
    arrived(qraw.at[other], mate_recv.at[1])
    make_bias(other)
    regroup(other)
    for which in (0, 1):
        arrived(kvbuf.at[X_TRANSIT, which], one_recv.at[0, which])
    pass_x.start()
    run(other, [0], [0], True)
    previous()
    run(core, [0], [0], True)
    arrived(kvbuf.at[1], pass_recv.at[0])
    before(3)
    for i in (2, 0, 1):
        along(i, 1).start()

    def half_stage(n, _):
        stage = n // 2
        t = jnp.where(lax.rem(n, 2) == 0, other, core)

        @pl.when(n == 1)
        def _():
            hand_on(0)

        @pl.when(n == 2)
        def _():
            hand_on(1)
            for cross in (0, 1):
                arrived(kvbuf.at[4 + cross], two_recv.at[0, cross])

        @pl.when(n == 4)
        def _():
            for cross in (0, 1):
                arrived(kvbuf.at[6 + cross], two_recv.at[1, cross])

        @pl.when(n == 6)
        def _():
            for cross in (0, 1):
                arrived(kvbuf.at[8 + cross], pass_recv.at[1 + cross])

        @pl.when(n == 7)
        def _():
            finish(other)
            remote(ostage.at[other], out_hbm.at[:, half(core), :],
                   mate_send.at[3], mate_recv.at[3], mate).start()

        left = jnp.where(stage == 0, 3 - 2 * side, 2 * stage + 2)
        right = jnp.where(stage == 0, 2, 2 * stage + 3)
        run(t, [2 * stage + 1, 2 * stage + 2], [left, right], False)
        return 0

    lax.fori_loop(0, 8, half_stage, 0)
    finish(core)
    own_out = pltpu.make_async_copy(ostage.at[core], out_hbm.at[:, half(core), :], here.at[0])
    own_out.start()
    for send in sends:
        send.wait_send()

    @pl.when(col < cols - 1)
    def _():
        for send in onward:
            send.wait_send()

    for i in range(3):
        for cross in (0, 1):
            along(i, cross).wait_send()
    pass_x.wait_send()
    for copy in pass_y:
        copy.wait_send()
    own_out.wait()
    remote(ostage.at[other], out_hbm.at[:, half(core), :],
           mate_send.at[3], mate_recv.at[3], mate).wait_send()
    arrived(out_hbm.at[:, half(other), :], mate_recv.at[3])


def local(queries, rotated_key_rows, value_matrix_rows, doc_start, block_keep):
    block = queries.shape[0]
    rows, cols = lax.axis_size("row"), lax.axis_size("col")
    kv = jnp.stack([rotated_key_rows, value_matrix_rows])
    kv = kv.reshape(2, block, 2, 2, 128).transpose(2, 0, 3, 1, 4)
    vmem = pl.BlockSpec(memory_space=pltpu.VMEM)
    hbm = pl.BlockSpec(memory_space=pl.ANY)
    return pl.pallas_call(
        functools.partial(kernel, rows, cols),
        out_shape=jax.ShapeDtypeStruct(queries.shape, BF16),
        in_specs=[hbm, vmem, vmem, pl.BlockSpec(memory_space=pltpu.SMEM)],
        out_specs=hbm,
        scratch_shapes=[
            pltpu.VMEM((13, 2, 2, 2, block, 128), BF16),
            pltpu.VMEM((2, 2, 2, block, 128), BF16),
            pltpu.VMEM((2, block, 16, 128), BF16),
            pltpu.VMEM((2, 24, 128), jnp.int32),
            pltpu.VMEM((2, 2, 128, block * 8), BF16),
            pltpu.VMEM((block, block * 8), BF16),
            pltpu.VMEM((2, CHUNKS, 2 * block, block), BF16),
            pltpu.VMEM((2, 2, 144, block * 8), F32),
            pltpu.VMEM((2, 2, 8, block * 8), F32),
            pltpu.VMEM((2, block, 16, 128), BF16),
            pltpu.SemaphoreType.DMA((3, 2)),
            pltpu.SemaphoreType.DMA((3, 2)),
            pltpu.SemaphoreType.DMA((3, 2)),
            pltpu.SemaphoreType.DMA((3, 2)),
            pltpu.SemaphoreType.DMA((3,)),
            pltpu.SemaphoreType.DMA((3,)),
            pltpu.SemaphoreType.DMA((4,)),
            pltpu.SemaphoreType.DMA((4,)),
            pltpu.SemaphoreType.DMA((2,)),
        ],
        compiler_params=pltpu.CompilerParams(
            collective_id=0, has_side_effects=True, vmem_limit_bytes=48 * 1024 * 1024),
        cost_estimate=pl.CostEstimate(flops=10**10, bytes_accessed=8 * 10**6, transcendentals=10**7),
    )(queries, kv, doc_start.reshape(1, block), block_keep)


def solution(mesh):
    return jax.shard_map(
        local,
        mesh=mesh,
        in_specs=(
            P(("col", "row"), None, None),
            P(("col", "row"), None, None),
            P(("col", "row"), None, None),
            P(("col", "row")),
            P(("col", "row"), None),
        ),
        out_specs=P(("col", "row"), None, None),
        check_vma=False,
    )
```

```python
import functools
import math

import jax
import jax.numpy as jnp
from jax import lax
from jax.experimental import pallas as pl
from jax.experimental.pallas import tpu as pltpu
from jax.sharding import PartitionSpec as P

MASKED = -1e30
STAGES = ((0,), (1, 2), (3, 4), (5, 6), (7, 8))
OFFSETS = (1, 3, 2)
X_TRANSIT, Y_TRANSIT = 10, 11
CHUNKS = 9
TILE = 256
F32, BF16 = jnp.float32, jnp.bfloat16


def kernel(rows, cols, q_hbm, kv_ref, start_ref, keep_ref, out_hbm,
           kvbuf, kvs, qraw, meta, qbuf, hot, bias, acc, top, sbuf, wbuf, ostage,
           one_send, one_recv, two_send, two_recv, pass_send, pass_recv,
           mate_send, mate_recv, here):
    block = q_hbm.shape[0]
    per_seg = rows // 2
    ring = per_seg // 2
    row, col = lax.axis_index("row"), lax.axis_index("col")
    core = lax.rem(row, 2)
    other = 1 - core
    place = row // 2
    side = lax.rem(place, 2)
    y = place // 2
    chip = col * per_seg + place
    next_col = lax.rem(col + 1, cols)
    last_col = lax.rem(col + cols - 1, cols)

    def device(seg, at_y, at_side, which):
        return {"row": (at_y * 2 + at_side) * 2 + which, "col": seg}

    mate = device(col, y, side, other)

    def beside(step, which):
        x = lax.rem(side * 2 + lax.rem(col, 2) + step + 4, 4)
        return device(col - lax.rem(col, 2) + lax.rem(x, 2), y, x // 2, which)

    def above(step):
        return device(col, lax.rem(y + step + ring, ring), side, core)

    way = 1 - 2 * core

    def remote(src, dst, send, recv, target):
        return pltpu.make_async_remote_copy(
            src_ref=src, dst_ref=dst, send_sem=send, recv_sem=recv,
            device_id=target, device_id_type=pl.DeviceIdType.MESH)

    def arrived(dst, sem):
        remote(dst, dst, mate_send.at[0], sem, mate).wait_recv()

    barrier = pltpu.get_barrier_semaphore()

    def greet(target):
        pl.semaphore_signal(barrier, inc=1, device_id=target, device_id_type=pl.DeviceIdType.MESH)

    greet(mate)
    for which in (0, 1):
        greet(beside(-way, which))

    @pl.when(col > 0)
    def _():
        for which in (0, 1):
            greet(device(last_col, y, side, which))
            greet(device(last_col, y, 1 - side, which))

    @pl.when(col == 0)
    def _():
        kvbuf[2:4] = jnp.zeros((2,) + kvbuf.shape[1:], BF16)

    greet(above(1))
    greet(above(-1))

    def half(which):
        return pl.ds(pl.multiple_of(which * 16, 16), 16)

    own_q = pltpu.make_async_copy(q_hbm.at[:, half(core), :], qraw.at[core], here.at[0])
    own_q.start()

    for which in (0, 1):
        for h in (0, 1):
            kvs[which, 0, h] = kv_ref[which, 0, h]
            kvs[which, 1, h] = kv_ref[which, 1, h].astype(F32).T.astype(BF16)
    own_kv = pltpu.make_async_copy(kvs.at[core], kvbuf.at[0, core], here.at[1])
    own_kv.start()

    backs = [0, 7 - 6 * side, 8]
    slots = [0, 3 - 2 * side, 2]
    for place_at, offset in enumerate(OFFSETS):
        backs += [2 * offset, 2 * offset - 1 + 2 * side]
        slots += [4 + 2 * place_at, 5 + 2 * place_at]

    own_block = chip * 2 + core
    for i in range(CHUNKS):
        for which in (0, 1):
            number = (chip - backs[i]) * 2 + which
            flag = keep_ref[0, jnp.maximum(number, 0)]
            flag = jnp.where(number == own_block, 1, flag)
            line = i * 2 + which
            meta[core, line:line + 1, :] = jnp.full((1, block), flag, jnp.int32)
    line = 2 * CHUNKS
    meta[core, line:line + 1, :] = start_ref[...]

    pl.semaphore_wait(barrier, jnp.where(col < cols - 1, 9, 5))

    sends = [
        remote(kvs.at[other], kvbuf.at[0, core], mate_send.at[2], mate_recv.at[2], mate),
        remote(meta.at[core], meta.at[core], mate_send.at[0], mate_recv.at[0], mate),
        remote(q_hbm.at[:, half(other), :], qraw.at[core], mate_send.at[1], mate_recv.at[1], mate),
    ]
    for which in (0, 1):
        sends.append(remote(kvs.at[which], kvbuf.at[X_TRANSIT, core],
                            one_send.at[0, which], one_recv.at[0, core],
                            beside(1 - 2 * which, which)))
    onward = []
    for slot, at_side in ((2, side), (3, 1 - side)):
        for which in (0, 1):
            onward.append(remote(kvs.at[which], kvbuf.at[slot, core],
                                 one_send.at[slot - 1, which], one_recv.at[slot - 1, core],
                                 device(next_col, y, at_side, which)))
    for send in sends:
        send.start()

    @pl.when(col < cols - 1)
    def _():
        for send in onward:
            send.start()

    def along(i, cross):
        offset = OFFSETS[i]
        held = y + offset < ring
        source = jnp.where(held, 0, 2) + cross
        to = (Y_TRANSIT if offset == 2 else 4 + 2 * i) + cross
        target = above(way) if offset == 2 else above(1 if offset == 1 else -1)
        return remote(kvbuf.at[source], kvbuf.at[to], two_send.at[i, cross], two_recv.at[i, cross],
                      target)

    pass_x = remote(kvbuf.at[X_TRANSIT], kvbuf.at[1], pass_send.at[0], pass_recv.at[0],
                    beside(way, core))
    pass_y = [remote(kvbuf.at[Y_TRANSIT + cross], kvbuf.at[8 + cross],
                     pass_send.at[1 + cross], pass_recv.at[1 + cross], above(way))
              for cross in (0, 1)]

    group = lax.broadcasted_iota(jnp.int32, hot.shape, 1) // 8
    token = lax.broadcasted_iota(jnp.int32, hot.shape, 0)
    hot[...] = jnp.where(group == token, 1.0, 0.0).astype(BF16)

    def make_bias(t):
        starts = meta[t, 2 * CHUNKS:2 * CHUNKS + 1, :]
        key_off = lax.broadcasted_iota(jnp.int32, (block, block), 0)
        query_pos = (chip * 2 + t) * block + lax.broadcasted_iota(jnp.int32, (block, block), 1)
        for i in range(CHUNKS):
            for which in (0, 1):
                key_pos = ((chip - backs[i]) * 2 + which) * block + key_off
                line = i * 2 + which
                flags = meta[t, line:line + 1, :]
                seen = (flags == 1) & (key_pos >= starts) & (key_pos <= query_pos)
                bias[t, i, which * block:(which + 1) * block, :] = (
                    jnp.where(seen, 0.0, MASKED).astype(BF16))

    def regroup(t):
        def piece(i, _):
            at = pl.ds(pl.multiple_of(i * 64, 64), 64)
            raw = qraw[t, at].astype(F32)
            to = pl.ds(pl.multiple_of(i * 512, 512), 512)
            qbuf[t, 0, :, to] = raw[:, :8, :].reshape(512, 128).T.astype(BF16)
            qbuf[t, 1, :, to] = raw[:, 8:, :].reshape(512, 128).T.astype(BF16)
            return 0
        lax.fori_loop(0, block // 64, piece, 0)

    scale = math.log2(math.e) / math.sqrt(128)
    tiles = block * 8 // TILE

    def run(stage, t):
        first, last = stage == 0, stage == len(STAGES) - 1
        used = STAGES[stage]
        span = len(used) * 2 * block
        ones = jnp.ones((16, span), BF16)
        units = [(r, h) for r in range(tiles) for h in (0, 1)]

        def score(n):
            r, h = units[n]
            at = slice(r * TILE, (r + 1) * TILE)
            rhs = jnp.concatenate([qbuf[t, h, :, at], hot[:, at]], axis=0)
            keys = jnp.concatenate(
                [kvbuf[slots[i], which, 0, h] for i in used for which in (0, 1)], axis=0)
            masks = jnp.concatenate([bias[t, i] for i in used], axis=0)
            scores = jnp.dot(jnp.concatenate([keys, masks], axis=1), rhs,
                             preferred_element_type=F32)
            sbuf[n % 2, :span] = scores
            return jnp.max(scores, axis=0, keepdims=True)

        done = []
        ready = score(0)
        for n, (r, h) in enumerate(units):
            at = slice(r * TILE, (r + 1) * TILE)
            new_top = ready
            if n + 1 < len(units):
                ready = score(n + 1)
            if not first:
                old_top = top[t, h, 0:1, at]
                new_top = jnp.maximum(old_top, new_top)
            wbuf[n % 2, :span] = jnp.exp2((sbuf[n % 2, :span] - new_top) * scale).astype(BF16)
            values = jnp.concatenate(
                [kvbuf[slots[i], which, 1, h] for i in used for which in (0, 1)], axis=1)
            total = jnp.dot(jnp.concatenate([values, ones], axis=0), wbuf[n % 2, :span],
                            preferred_element_type=F32)
            if not first:
                total = total + acc[t, h, :, at] * jnp.exp2((old_top - new_top) * scale)
            if last:
                result = total[:128] / total[128:129]
                done.append(result.T.reshape(TILE // 8, 8, 128))
                if h == 1:
                    both = jnp.concatenate(done[-2:], axis=1).astype(BF16)
                    ostage[t, r * (TILE // 8):(r + 1) * (TILE // 8)] = both
            else:
                acc[t, h, :, at] = total
                top[t, h, 0:1, at] = new_top

    def run_both(stage, between=None):
        def step(t, _):
            run(stage, t)
            if between is not None:
                @pl.when(t == 0)
                def _():
                    between()
            return 0
        lax.fori_loop(0, 2, step, 0)

    def start_own(early):
        for i in (2, 0, 1):
            held = y + OFFSETS[i] < ring

            @pl.when(held if early else jnp.logical_not(held))
            def _():
                along(i, 0).start()

    def hand_on(cross):
        arrived(kvbuf.at[Y_TRANSIT + cross], two_recv.at[2, cross])
        pass_y[cross].start()

    def before(slot):
        @pl.when(col > 0)
        def _():
            for which in (0, 1):
                arrived(kvbuf.at[slot, which], one_recv.at[slot - 1, which])

    def previous():
        before(2)
        start_own(False)

    make_bias(core)
    own_q.wait()
    regroup(core)
    own_kv.wait()
    arrived(kvbuf.at[0, other], mate_recv.at[2])
    start_own(True)
    arrived(meta.at[other], mate_recv.at[0])
    arrived(qraw.at[other], mate_recv.at[1])
    make_bias(other)
    regroup(other)
    for which in (0, 1):
        arrived(kvbuf.at[X_TRANSIT, which], one_recv.at[0, which])
    pass_x.start()
    run_both(0, previous)
    arrived(kvbuf.at[1], pass_recv.at[0])
    before(3)
    for i in (2, 0, 1):
        along(i, 1).start()
    run_both(1, lambda: hand_on(0))
    hand_on(1)
    for stage in (2, 3):
        for cross in (0, 1):
            arrived(kvbuf.at[2 * stage + cross], two_recv.at[stage - 2, cross])
        run_both(stage)
    for cross in (0, 1):
        arrived(kvbuf.at[8 + cross], pass_recv.at[1 + cross])

    def finish(t, _):
        t = jnp.where(t == 0, other, core)
        run(4, t)

        @pl.when(t == other)
        def _():
            remote(ostage.at[other], out_hbm.at[:, half(core), :],
                   mate_send.at[3], mate_recv.at[3], mate).start()
        return 0

    lax.fori_loop(0, 2, finish, 0)
    own_out = pltpu.make_async_copy(ostage.at[core], out_hbm.at[:, half(core), :], here.at[0])
    own_out.start()
    for send in sends:
        send.wait_send()

    @pl.when(col < cols - 1)
    def _():
        for send in onward:
            send.wait_send()

    for i in range(3):
        for cross in (0, 1):
            along(i, cross).wait_send()
    pass_x.wait_send()
    for copy in pass_y:
        copy.wait_send()
    own_out.wait()
    remote(ostage.at[other], out_hbm.at[:, half(core), :],
           mate_send.at[3], mate_recv.at[3], mate).wait_send()
    arrived(out_hbm.at[:, half(other), :], mate_recv.at[3])


def local(queries, rotated_key_rows, value_matrix_rows, doc_start, block_keep):
    block = queries.shape[0]
    rows, cols = lax.axis_size("row"), lax.axis_size("col")
    kv = jnp.stack([rotated_key_rows, value_matrix_rows])
    kv = kv.reshape(2, block, 2, 2, 128).transpose(2, 0, 3, 1, 4)
    vmem = pl.BlockSpec(memory_space=pltpu.VMEM)
    hbm = pl.BlockSpec(memory_space=pl.ANY)
    return pl.pallas_call(
        functools.partial(kernel, rows, cols),
        out_shape=jax.ShapeDtypeStruct(queries.shape, BF16),
        in_specs=[hbm, vmem, vmem, pl.BlockSpec(memory_space=pltpu.SMEM)],
        out_specs=hbm,
        scratch_shapes=[
            pltpu.VMEM((13, 2, 2, 2, block, 128), BF16),
            pltpu.VMEM((2, 2, 2, block, 128), BF16),
            pltpu.VMEM((2, block, 16, 128), BF16),
            pltpu.VMEM((2, 24, 128), jnp.int32),
            pltpu.VMEM((2, 2, 128, block * 8), BF16),
            pltpu.VMEM((block, block * 8), BF16),
            pltpu.VMEM((2, CHUNKS, 2 * block, block), BF16),
            pltpu.VMEM((2, 2, 144, block * 8), F32),
            pltpu.VMEM((2, 2, 8, block * 8), F32),
            pltpu.VMEM((2, 4 * block, TILE), F32),
            pltpu.VMEM((2, 4 * block, TILE), BF16),
            pltpu.VMEM((2, block, 16, 128), BF16),
            pltpu.SemaphoreType.DMA((3, 2)),
            pltpu.SemaphoreType.DMA((3, 2)),
            pltpu.SemaphoreType.DMA((3, 2)),
            pltpu.SemaphoreType.DMA((3, 2)),
            pltpu.SemaphoreType.DMA((3,)),
            pltpu.SemaphoreType.DMA((3,)),
            pltpu.SemaphoreType.DMA((4,)),
            pltpu.SemaphoreType.DMA((4,)),
            pltpu.SemaphoreType.DMA((2,)),
        ],
        compiler_params=pltpu.CompilerParams(
            collective_id=0, has_side_effects=True, vmem_limit_bytes=48 * 1024 * 1024),
        cost_estimate=pl.CostEstimate(flops=10**10, bytes_accessed=8 * 10**6, transcendentals=10**7),
    )(queries, kv, doc_start.reshape(1, block), block_keep)


def solution(mesh):
    return jax.shard_map(
        local,
        mesh=mesh,
        in_specs=(
            P(("col", "row"), None, None),
            P(("col", "row"), None, None),
            P(("col", "row"), None, None),
            P(("col", "row")),
            P(("col", "row"), None),
        ),
        out_specs=P(("col", "row"), None, None),
        check_vma=False,
    )
```

```python
import functools
import math

import jax
import jax.numpy as jnp
from jax import lax
from jax.experimental import pallas as pl
from jax.experimental.pallas import tpu as pltpu
from jax.sharding import PartitionSpec as P

MASKED = -1e30
STAGES = ((0,), (1, 2), (3, 5), (7, 4), (6, 8))
OFFSETS = (1, 3, 2)
X_TRANSIT, Y_TRANSIT, LATE_TRANSIT = 10, 11, 12
CHUNKS = 9
TILE = 256
F32, BF16 = jnp.float32, jnp.bfloat16


def kernel(rows, cols, q_hbm, kv_ref, start_ref, keep_ref, out_hbm,
           kvbuf, kvs, qraw, meta, qbuf, hot, bias, acc, top, sbuf, wbuf, ostage,
           one_send, one_recv, two_send, two_recv, pass_send, pass_recv,
           mate_send, mate_recv, here):
    block = q_hbm.shape[0]
    per_seg = rows // 2
    ring = per_seg // 2
    row, col = lax.axis_index("row"), lax.axis_index("col")
    core = lax.rem(row, 2)
    other = 1 - core
    place = row // 2
    side = lax.rem(place, 2)
    y = place // 2
    chip = col * per_seg + place
    next_col = lax.rem(col + 1, cols)
    last_col = lax.rem(col + cols - 1, cols)

    def device(seg, at_y, at_side, which):
        return {"row": (at_y * 2 + at_side) * 2 + which, "col": seg}

    mate = device(col, y, side, other)

    def beside(step, which):
        x = lax.rem(side * 2 + lax.rem(col, 2) + step + 4, 4)
        return device(col - lax.rem(col, 2) + lax.rem(x, 2), y, x // 2, which)

    def above(step):
        return device(col, lax.rem(y + step + ring, ring), side, core)

    way = 1 - 2 * core

    def remote(src, dst, send, recv, target):
        return pltpu.make_async_remote_copy(
            src_ref=src, dst_ref=dst, send_sem=send, recv_sem=recv,
            device_id=target, device_id_type=pl.DeviceIdType.MESH)

    def arrived(dst, sem):
        remote(dst, dst, mate_send.at[0], sem, mate).wait_recv()

    barrier = pltpu.get_barrier_semaphore()

    def greet(target):
        pl.semaphore_signal(barrier, inc=1, device_id=target, device_id_type=pl.DeviceIdType.MESH)

    greet(mate)
    for which in (0, 1):
        greet(beside(-way, which))

    @pl.when(col > 0)
    def _():
        for which in (0, 1):
            greet(device(last_col, y, side, which))
            greet(device(last_col, y, 1 - side, which))

    @pl.when(col == 0)
    def _():
        kvbuf[2:4] = jnp.zeros((2,) + kvbuf.shape[1:], BF16)

    greet(above(1))
    greet(above(-1))

    def half(which):
        return pl.ds(pl.multiple_of(which * 16, 16), 16)

    own_q = pltpu.make_async_copy(q_hbm.at[:, half(core), :], qraw.at[core], here.at[0])
    own_q.start()

    for which in (0, 1):
        for h in (0, 1):
            kvs[which, 0, h] = kv_ref[which, 0, h]
            kvs[which, 1, h] = kv_ref[which, 1, h].astype(F32).T.astype(BF16)
    own_kv = pltpu.make_async_copy(kvs.at[core], kvbuf.at[0, core], here.at[1])
    own_kv.start()

    backs = [0, 7 - 6 * side, 8]
    slots = [0, 3 - 2 * side, 2]
    for place_at, offset in enumerate(OFFSETS):
        backs += [2 * offset, 2 * offset - 1 + 2 * side]
        slots += [4 + 2 * place_at, 5 + 2 * place_at]

    own_block = chip * 2 + core
    for i in range(CHUNKS):
        for which in (0, 1):
            number = (chip - backs[i]) * 2 + which
            flag = keep_ref[0, jnp.maximum(number, 0)]
            flag = jnp.where(number == own_block, 1, flag)
            line = i * 2 + which
            meta[core, line:line + 1, :] = jnp.full((1, block), flag, jnp.int32)
    line = 2 * CHUNKS
    meta[core, line:line + 1, :] = start_ref[...]

    pl.semaphore_wait(barrier, jnp.where(col < cols - 1, 9, 5))

    sends = [
        remote(kvs.at[other], kvbuf.at[0, core], mate_send.at[2], mate_recv.at[2], mate),
        remote(meta.at[core], meta.at[core], mate_send.at[0], mate_recv.at[0], mate),
        remote(q_hbm.at[:, half(other), :], qraw.at[core], mate_send.at[1], mate_recv.at[1], mate),
    ]
    for which in (0, 1):
        sends.append(remote(kvs.at[which], kvbuf.at[X_TRANSIT, core],
                            one_send.at[0, which], one_recv.at[0, core],
                            beside(1 - 2 * which, which)))
    onward = []
    for slot, at_side in ((2, side), (3, 1 - side)):
        for which in (0, 1):
            onward.append(remote(kvs.at[which], kvbuf.at[slot, core],
                                 one_send.at[slot - 1, which], one_recv.at[slot - 1, core],
                                 device(next_col, y, at_side, which)))
    for send in sends:
        send.start()

    @pl.when(col < cols - 1)
    def _():
        for send in onward:
            send.start()

    def along(i, cross):
        offset = OFFSETS[i]
        held = y + offset < ring
        source = jnp.where(held, 0, 2) + cross
        to = (Y_TRANSIT if offset == 2 else 4 + 2 * i) + cross
        target = above(way) if offset == 2 else above(1 if offset == 1 else -1)
        return remote(kvbuf.at[source], kvbuf.at[to], two_send.at[i, cross], two_recv.at[i, cross],
                      target)

    pass_x = remote(kvbuf.at[X_TRANSIT], kvbuf.at[1], pass_send.at[0], pass_recv.at[0],
                    beside(way, core))
    pass_y = remote(kvbuf.at[Y_TRANSIT], kvbuf.at[8], pass_send.at[1], pass_recv.at[1], above(way))
    late = remote(kvbuf.at[8], kvbuf.at[LATE_TRANSIT], two_send.at[2, 1], two_recv.at[2, 1],
                  beside(way, core))
    pass_late = remote(kvbuf.at[LATE_TRANSIT], kvbuf.at[9], pass_send.at[2], pass_recv.at[2],
                       beside(way, core))

    group = lax.broadcasted_iota(jnp.int32, hot.shape, 1) // 8
    token = lax.broadcasted_iota(jnp.int32, hot.shape, 0)
    hot[...] = jnp.where(group == token, 1.0, 0.0).astype(BF16)

    def make_bias(t):
        starts = meta[t, 2 * CHUNKS:2 * CHUNKS + 1, :]
        key_off = lax.broadcasted_iota(jnp.int32, (block, block), 0)
        query_pos = (chip * 2 + t) * block + lax.broadcasted_iota(jnp.int32, (block, block), 1)
        for i in range(CHUNKS):
            for which in (0, 1):
                key_pos = ((chip - backs[i]) * 2 + which) * block + key_off
                line = i * 2 + which
                flags = meta[t, line:line + 1, :]
                seen = (flags == 1) & (key_pos >= starts) & (key_pos <= query_pos)
                bias[t, i, which * block:(which + 1) * block, :] = (
                    jnp.where(seen, 0.0, MASKED).astype(BF16))

    def regroup(t):
        def piece(i, _):
            at = pl.ds(pl.multiple_of(i * 64, 64), 64)
            raw = qraw[t, at].astype(F32)
            to = pl.ds(pl.multiple_of(i * 512, 512), 512)
            qbuf[t, 0, :, to] = raw[:, :8, :].reshape(512, 128).T.astype(BF16)
            qbuf[t, 1, :, to] = raw[:, 8:, :].reshape(512, 128).T.astype(BF16)
            return 0
        lax.fori_loop(0, block // 64, piece, 0)

    scale = math.log2(math.e) / math.sqrt(128)
    tiles = block * 8 // TILE

    def run(stage, t):
        first, last = stage == 0, stage == len(STAGES) - 1
        used = STAGES[stage]
        span = len(used) * 2 * block
        ones = jnp.ones((16, span), BF16)
        units = [(r, h) for r in range(tiles) for h in (0, 1)]

        def score(n):
            r, h = units[n]
            at = slice(r * TILE, (r + 1) * TILE)
            rhs = jnp.concatenate([qbuf[t, h, :, at], hot[:, at]], axis=0)
            keys = jnp.concatenate(
                [kvbuf[slots[i], which, 0, h] for i in used for which in (0, 1)], axis=0)
            masks = jnp.concatenate([bias[t, i] for i in used], axis=0)
            scores = jnp.dot(jnp.concatenate([keys, masks], axis=1), rhs,
                             preferred_element_type=F32)
            sbuf[n % 2, :span] = scores
            return jnp.max(scores, axis=0, keepdims=True)

        done = []
        ready = score(0)
        for n, (r, h) in enumerate(units):
            at = slice(r * TILE, (r + 1) * TILE)
            new_top = ready
            if n + 1 < len(units):
                ready = score(n + 1)
            if not first:
                old_top = top[t, h, 0:1, at]
                new_top = jnp.maximum(old_top, new_top)
            wbuf[n % 2, :span] = jnp.exp2((sbuf[n % 2, :span] - new_top) * scale).astype(BF16)
            values = jnp.concatenate(
                [kvbuf[slots[i], which, 1, h] for i in used for which in (0, 1)], axis=1)
            total = jnp.dot(jnp.concatenate([values, ones], axis=0), wbuf[n % 2, :span],
                            preferred_element_type=F32)
            if not first:
                total = total + acc[t, h, :, at] * jnp.exp2((old_top - new_top) * scale)
            if last:
                result = total[:128] / total[128:129]
                done.append(result.T.reshape(TILE // 8, 8, 128))
                if h == 1:
                    both = jnp.concatenate(done[-2:], axis=1).astype(BF16)
                    ostage[t, r * (TILE // 8):(r + 1) * (TILE // 8)] = both
            else:
                acc[t, h, :, at] = total
                top[t, h, 0:1, at] = new_top

    def run_both(stage, between=None):
        def step(t, _):
            run(stage, t)
            if between is not None:
                @pl.when(t == 0)
                def _():
                    between()
            return 0
        lax.fori_loop(0, 2, step, 0)

    def start_own(early):
        for i in (2, 0, 1):
            held = y + OFFSETS[i] < ring

            @pl.when(held if early else jnp.logical_not(held))
            def _():
                along(i, 0).start()

    def far():
        arrived(kvbuf.at[Y_TRANSIT], two_recv.at[2, 0])
        pass_y.start()

    def far_here():
        arrived(kvbuf.at[8], pass_recv.at[1])
        late.start()

    def far_on():
        arrived(kvbuf.at[LATE_TRANSIT], two_recv.at[2, 1])
        pass_late.start()

    def before(slot):
        @pl.when(col > 0)
        def _():
            for which in (0, 1):
                arrived(kvbuf.at[slot, which], one_recv.at[slot - 1, which])

    def previous():
        before(2)
        start_own(False)

    make_bias(core)
    own_q.wait()
    regroup(core)
    own_kv.wait()
    arrived(kvbuf.at[0, other], mate_recv.at[2])
    start_own(True)
    arrived(meta.at[other], mate_recv.at[0])
    arrived(qraw.at[other], mate_recv.at[1])
    make_bias(other)
    regroup(other)
    for which in (0, 1):
        arrived(kvbuf.at[X_TRANSIT, which], one_recv.at[0, which])
    pass_x.start()
    run_both(0, previous)
    arrived(kvbuf.at[1], pass_recv.at[0])
    before(3)
    for i in (0, 1):
        along(i, 1).start()
    run_both(1, far)
    for i in (0, 1):
        arrived(kvbuf.at[4 + 2 * i], two_recv.at[i, 0])
    run_both(2, far_here)
    arrived(kvbuf.at[5], two_recv.at[0, 1])
    run_both(3, far_on)
    arrived(kvbuf.at[7], two_recv.at[1, 1])
    arrived(kvbuf.at[9], pass_recv.at[2])

    def finish(t, _):
        t = jnp.where(t == 0, other, core)
        run(4, t)

        @pl.when(t == other)
        def _():
            remote(ostage.at[other], out_hbm.at[:, half(core), :],
                   mate_send.at[3], mate_recv.at[3], mate).start()
        return 0

    lax.fori_loop(0, 2, finish, 0)
    own_out = pltpu.make_async_copy(ostage.at[core], out_hbm.at[:, half(core), :], here.at[0])
    own_out.start()
    for send in sends:
        send.wait_send()

    @pl.when(col < cols - 1)
    def _():
        for send in onward:
            send.wait_send()

    for i in range(3):
        along(i, 0).wait_send()
        if i < 2:
            along(i, 1).wait_send()
    for copy in (pass_x, pass_y, late, pass_late):
        copy.wait_send()
    own_out.wait()
    remote(ostage.at[other], out_hbm.at[:, half(core), :],
           mate_send.at[3], mate_recv.at[3], mate).wait_send()
    arrived(out_hbm.at[:, half(other), :], mate_recv.at[3])


def local(queries, rotated_key_rows, value_matrix_rows, doc_start, block_keep):
    block = queries.shape[0]
    rows, cols = lax.axis_size("row"), lax.axis_size("col")
    kv = jnp.stack([rotated_key_rows, value_matrix_rows])
    kv = kv.reshape(2, block, 2, 2, 128).transpose(2, 0, 3, 1, 4)
    vmem = pl.BlockSpec(memory_space=pltpu.VMEM)
    hbm = pl.BlockSpec(memory_space=pl.ANY)
    return pl.pallas_call(
        functools.partial(kernel, rows, cols),
        out_shape=jax.ShapeDtypeStruct(queries.shape, BF16),
        in_specs=[hbm, vmem, vmem, pl.BlockSpec(memory_space=pltpu.SMEM)],
        out_specs=hbm,
        scratch_shapes=[
            pltpu.VMEM((13, 2, 2, 2, block, 128), BF16),
            pltpu.VMEM((2, 2, 2, block, 128), BF16),
            pltpu.VMEM((2, block, 16, 128), BF16),
            pltpu.VMEM((2, 24, 128), jnp.int32),
            pltpu.VMEM((2, 2, 128, block * 8), BF16),
            pltpu.VMEM((block, block * 8), BF16),
            pltpu.VMEM((2, CHUNKS, 2 * block, block), BF16),
            pltpu.VMEM((2, 2, 144, block * 8), F32),
            pltpu.VMEM((2, 2, 8, block * 8), F32),
            pltpu.VMEM((2, 4 * block, TILE), F32),
            pltpu.VMEM((2, 4 * block, TILE), BF16),
            pltpu.VMEM((2, block, 16, 128), BF16),
            pltpu.SemaphoreType.DMA((3, 2)),
            pltpu.SemaphoreType.DMA((3, 2)),
            pltpu.SemaphoreType.DMA((3, 2)),
            pltpu.SemaphoreType.DMA((3, 2)),
            pltpu.SemaphoreType.DMA((3,)),
            pltpu.SemaphoreType.DMA((3,)),
            pltpu.SemaphoreType.DMA((4,)),
            pltpu.SemaphoreType.DMA((4,)),
            pltpu.SemaphoreType.DMA((2,)),
        ],
        compiler_params=pltpu.CompilerParams(
            collective_id=0, has_side_effects=True, vmem_limit_bytes=48 * 1024 * 1024),
        cost_estimate=pl.CostEstimate(flops=10**10, bytes_accessed=8 * 10**6, transcendentals=10**7),
    )(queries, kv, doc_start.reshape(1, block), block_keep)


def solution(mesh):
    return jax.shard_map(
        local,
        mesh=mesh,
        in_specs=(
            P(("col", "row"), None, None),
            P(("col", "row"), None, None),
            P(("col", "row"), None, None),
            P(("col", "row")),
            P(("col", "row"), None),
        ),
        out_specs=P(("col", "row"), None, None),
        check_vma=False,
    )
```

```python
import functools
import math

import jax
import jax.numpy as jnp
from jax import lax
from jax.experimental import pallas as pl
from jax.experimental.pallas import tpu as pltpu
from jax.sharding import PartitionSpec as P

MASKED = -1e30
STAGES = ((0,), (2,), (1, 3), (5, 4), (6, 7), (8,))
OFFSETS = (1, 3, 2)
X_TRANSIT, Y_TRANSIT = 10, 11
CHUNKS = 9
TILE = 256
F32, BF16 = jnp.float32, jnp.bfloat16


def kernel(rows, cols, q_hbm, kv_ref, start_ref, keep_ref, out_hbm,
           kvbuf, kvs, qraw, meta, qbuf, hot, bias, acc, top, sbuf, wbuf, ostage,
           one_send, one_recv, two_send, two_recv, pass_send, pass_recv,
           mate_send, mate_recv, here):
    block = q_hbm.shape[0]
    per_seg = rows // 2
    ring = per_seg // 2
    row, col = lax.axis_index("row"), lax.axis_index("col")
    core = lax.rem(row, 2)
    other = 1 - core
    place = row // 2
    side = lax.rem(place, 2)
    y = place // 2
    chip = col * per_seg + place
    next_col = lax.rem(col + 1, cols)
    last_col = lax.rem(col + cols - 1, cols)

    def device(seg, at_y, at_side, which):
        return {"row": (at_y * 2 + at_side) * 2 + which, "col": seg}

    mate = device(col, y, side, other)

    def beside(step, which):
        x = lax.rem(side * 2 + lax.rem(col, 2) + step + 4, 4)
        return device(col - lax.rem(col, 2) + lax.rem(x, 2), y, x // 2, which)

    def above(step):
        return device(col, lax.rem(y + step + ring, ring), side, core)

    way = 1 - 2 * core

    def remote(src, dst, send, recv, target):
        return pltpu.make_async_remote_copy(
            src_ref=src, dst_ref=dst, send_sem=send, recv_sem=recv,
            device_id=target, device_id_type=pl.DeviceIdType.MESH)

    def arrived(dst, sem):
        remote(dst, dst, mate_send.at[0], sem, mate).wait_recv()

    barrier = pltpu.get_barrier_semaphore()

    def greet(target):
        pl.semaphore_signal(barrier, inc=1, device_id=target, device_id_type=pl.DeviceIdType.MESH)

    greet(mate)
    for which in (0, 1):
        greet(beside(-way, which))

    @pl.when(col > 0)
    def _():
        for which in (0, 1):
            greet(device(last_col, y, side, which))
            greet(device(last_col, y, 1 - side, which))

    @pl.when(col == 0)
    def _():
        kvbuf[2:4] = jnp.zeros((2,) + kvbuf.shape[1:], BF16)

    greet(above(1))
    greet(above(-1))

    def half(which):
        return pl.ds(pl.multiple_of(which * 16, 16), 16)

    own_q = pltpu.make_async_copy(q_hbm.at[:, half(core), :], qraw.at[core], here.at[0])
    own_q.start()

    for which in (0, 1):
        for h in (0, 1):
            kvs[which, 0, h] = kv_ref[which, 0, h]
            kvs[which, 1, h] = kv_ref[which, 1, h].astype(F32).T.astype(BF16)
    own_kv = pltpu.make_async_copy(kvs.at[core], kvbuf.at[0, core], here.at[1])
    own_kv.start()

    backs = [0, 7 - 6 * side, 8]
    slots = [0, 3 - 2 * side, 2]
    for place_at, offset in enumerate(OFFSETS):
        backs += [2 * offset, 2 * offset - 1 + 2 * side]
        slots += [4 + 2 * place_at, 5 + 2 * place_at]

    own_block = chip * 2 + core
    for i in range(CHUNKS):
        for which in (0, 1):
            number = (chip - backs[i]) * 2 + which
            flag = keep_ref[0, jnp.maximum(number, 0)]
            flag = jnp.where(number == own_block, 1, flag)
            line = i * 2 + which
            meta[core, line:line + 1, :] = jnp.full((1, block), flag, jnp.int32)
    line = 2 * CHUNKS
    meta[core, line:line + 1, :] = start_ref[...]

    pl.semaphore_wait(barrier, jnp.where(col < cols - 1, 9, 5))

    sends = [
        remote(kvs.at[other], kvbuf.at[0, core], mate_send.at[2], mate_recv.at[2], mate),
        remote(meta.at[core], meta.at[core], mate_send.at[0], mate_recv.at[0], mate),
        remote(q_hbm.at[:, half(other), :], qraw.at[core], mate_send.at[1], mate_recv.at[1], mate),
    ]
    for which in (0, 1):
        sends.append(remote(kvs.at[which], kvbuf.at[X_TRANSIT, core],
                            one_send.at[0, which], one_recv.at[0, core],
                            beside(1 - 2 * which, which)))
    onward = []
    for slot, at_side in ((2, side), (3, 1 - side)):
        for which in (0, 1):
            onward.append(remote(kvs.at[which], kvbuf.at[slot, core],
                                 one_send.at[slot - 1, which], one_recv.at[slot - 1, core],
                                 device(next_col, y, at_side, which)))
    for send in sends:
        send.start()

    @pl.when(col < cols - 1)
    def _():
        for send in onward:
            send.start()

    def along(i, cross):
        offset = OFFSETS[i]
        held = y + offset < ring
        source = jnp.where(held, 0, 2) + cross
        to = (Y_TRANSIT if offset == 2 else 4 + 2 * i) + cross
        target = above(way) if offset == 2 else above(1 if offset == 1 else -1)
        return remote(kvbuf.at[source], kvbuf.at[to], two_send.at[i, cross], two_recv.at[i, cross],
                      target)

    pass_x = remote(kvbuf.at[X_TRANSIT], kvbuf.at[1], pass_send.at[0], pass_recv.at[0],
                    beside(way, core))
    pass_y = [remote(kvbuf.at[Y_TRANSIT + cross], kvbuf.at[8 + cross],
                     pass_send.at[1 + cross], pass_recv.at[1 + cross], above(way))
              for cross in (0, 1)]

    group = lax.broadcasted_iota(jnp.int32, hot.shape, 1) // 8
    token = lax.broadcasted_iota(jnp.int32, hot.shape, 0)
    hot[...] = jnp.where(group == token, 1.0, 0.0).astype(BF16)

    def make_bias(t):
        starts = meta[t, 2 * CHUNKS:2 * CHUNKS + 1, :]
        key_off = lax.broadcasted_iota(jnp.int32, (block, block), 0)
        query_pos = (chip * 2 + t) * block + lax.broadcasted_iota(jnp.int32, (block, block), 1)
        for i in range(CHUNKS):
            for which in (0, 1):
                key_pos = ((chip - backs[i]) * 2 + which) * block + key_off
                line = i * 2 + which
                flags = meta[t, line:line + 1, :]
                seen = (flags == 1) & (key_pos >= starts) & (key_pos <= query_pos)
                bias[t, i, which * block:(which + 1) * block, :] = (
                    jnp.where(seen, 0.0, MASKED).astype(BF16))

    def regroup(t):
        def piece(i, _):
            at = pl.ds(pl.multiple_of(i * 64, 64), 64)
            raw = qraw[t, at].astype(F32)
            to = pl.ds(pl.multiple_of(i * 512, 512), 512)
            qbuf[t, 0, :, to] = raw[:, :8, :].reshape(512, 128).T.astype(BF16)
            qbuf[t, 1, :, to] = raw[:, 8:, :].reshape(512, 128).T.astype(BF16)
            return 0
        lax.fori_loop(0, block // 64, piece, 0)

    scale = math.log2(math.e) / math.sqrt(128)
    tiles = block * 8 // TILE

    def run(stage, t):
        first, last = stage == 0, stage == len(STAGES) - 1
        used = STAGES[stage]
        span = len(used) * 2 * block
        ones = jnp.ones((16, span), BF16)
        units = [(r, h) for r in range(tiles) for h in (0, 1)]

        def score(n):
            r, h = units[n]
            at = slice(r * TILE, (r + 1) * TILE)
            rhs = jnp.concatenate([qbuf[t, h, :, at], hot[:, at]], axis=0)
            keys = jnp.concatenate(
                [kvbuf[slots[i], which, 0, h] for i in used for which in (0, 1)], axis=0)
            masks = jnp.concatenate([bias[t, i] for i in used], axis=0)
            scores = jnp.dot(jnp.concatenate([keys, masks], axis=1), rhs,
                             preferred_element_type=F32)
            sbuf[n % 2, :span] = scores
            return jnp.max(scores, axis=0, keepdims=True)

        done = []
        ready = score(0)
        for n, (r, h) in enumerate(units):
            at = slice(r * TILE, (r + 1) * TILE)
            new_top = ready
            if n + 1 < len(units):
                ready = score(n + 1)
            if not first:
                old_top = top[t, h, 0:1, at]
                new_top = jnp.maximum(old_top, new_top)
            wbuf[n % 2, :span] = jnp.exp2((sbuf[n % 2, :span] - new_top) * scale).astype(BF16)
            values = jnp.concatenate(
                [kvbuf[slots[i], which, 1, h] for i in used for which in (0, 1)], axis=1)
            total = jnp.dot(jnp.concatenate([values, ones], axis=0), wbuf[n % 2, :span],
                            preferred_element_type=F32)
            if not first:
                total = total + acc[t, h, :, at] * jnp.exp2((old_top - new_top) * scale)
            if last:
                result = total[:128] / total[128:129]
                done.append(result.T.reshape(TILE // 8, 8, 128))
                if h == 1:
                    both = jnp.concatenate(done[-2:], axis=1).astype(BF16)
                    ostage[t, r * (TILE // 8):(r + 1) * (TILE // 8)] = both
            else:
                acc[t, h, :, at] = total
                top[t, h, 0:1, at] = new_top

    def run_both(stage, between=None):
        def step(t, _):
            run(stage, t)
            if between is not None:
                @pl.when(t == 0)
                def _():
                    between()
            return 0
        lax.fori_loop(0, 2, step, 0)

    def start_own(early):
        for i in (2, 0, 1):
            held = y + OFFSETS[i] < ring

            @pl.when(held if early else jnp.logical_not(held))
            def _():
                along(i, 0).start()

    def hand_on(cross):
        arrived(kvbuf.at[Y_TRANSIT + cross], two_recv.at[2, cross])
        pass_y[cross].start()

    def before(slot):
        @pl.when(col > 0)
        def _():
            for which in (0, 1):
                arrived(kvbuf.at[slot, which], one_recv.at[slot - 1, which])

    def previous():
        before(2)
        start_own(False)

    make_bias(core)
    own_q.wait()
    regroup(core)
    own_kv.wait()
    arrived(kvbuf.at[0, other], mate_recv.at[2])
    start_own(True)
    arrived(meta.at[other], mate_recv.at[0])
    arrived(qraw.at[other], mate_recv.at[1])
    make_bias(other)
    regroup(other)
    def across():
        for which in (0, 1):
            arrived(kvbuf.at[X_TRANSIT, which], one_recv.at[0, which])
        pass_x.start()

    run_both(0, across)
    previous()
    run_both(1)
    arrived(kvbuf.at[1], pass_recv.at[0])
    before(3)
    for i in (2, 0, 1):
        along(i, 1).start()
    arrived(kvbuf.at[4], two_recv.at[0, 0])
    run_both(2, lambda: hand_on(0))
    hand_on(1)
    arrived(kvbuf.at[6], two_recv.at[1, 0])
    arrived(kvbuf.at[5], two_recv.at[0, 1])
    run_both(3)
    arrived(kvbuf.at[7], two_recv.at[1, 1])
    arrived(kvbuf.at[8], pass_recv.at[1])
    run_both(4)
    arrived(kvbuf.at[9], pass_recv.at[2])

    def finish(t, _):
        t = jnp.where(t == 0, other, core)
        run(5, t)

        @pl.when(t == other)
        def _():
            remote(ostage.at[other], out_hbm.at[:, half(core), :],
                   mate_send.at[3], mate_recv.at[3], mate).start()
        return 0

    lax.fori_loop(0, 2, finish, 0)
    own_out = pltpu.make_async_copy(ostage.at[core], out_hbm.at[:, half(core), :], here.at[0])
    own_out.start()
    for send in sends:
        send.wait_send()

    @pl.when(col < cols - 1)
    def _():
        for send in onward:
            send.wait_send()

    for i in range(3):
        for cross in (0, 1):
            along(i, cross).wait_send()
    pass_x.wait_send()
    for copy in pass_y:
        copy.wait_send()
    own_out.wait()
    remote(ostage.at[other], out_hbm.at[:, half(core), :],
           mate_send.at[3], mate_recv.at[3], mate).wait_send()
    arrived(out_hbm.at[:, half(other), :], mate_recv.at[3])


def local(queries, rotated_key_rows, value_matrix_rows, doc_start, block_keep):
    block = queries.shape[0]
    rows, cols = lax.axis_size("row"), lax.axis_size("col")
    kv = jnp.stack([rotated_key_rows, value_matrix_rows])
    kv = kv.reshape(2, block, 2, 2, 128).transpose(2, 0, 3, 1, 4)
    vmem = pl.BlockSpec(memory_space=pltpu.VMEM)
    hbm = pl.BlockSpec(memory_space=pl.ANY)
    return pl.pallas_call(
        functools.partial(kernel, rows, cols),
        out_shape=jax.ShapeDtypeStruct(queries.shape, BF16),
        in_specs=[hbm, vmem, vmem, pl.BlockSpec(memory_space=pltpu.SMEM)],
        out_specs=hbm,
        scratch_shapes=[
            pltpu.VMEM((13, 2, 2, 2, block, 128), BF16),
            pltpu.VMEM((2, 2, 2, block, 128), BF16),
            pltpu.VMEM((2, block, 16, 128), BF16),
            pltpu.VMEM((2, 24, 128), jnp.int32),
            pltpu.VMEM((2, 2, 128, block * 8), BF16),
            pltpu.VMEM((block, block * 8), BF16),
            pltpu.VMEM((2, CHUNKS, 2 * block, block), BF16),
            pltpu.VMEM((2, 2, 144, block * 8), F32),
            pltpu.VMEM((2, 2, 8, block * 8), F32),
            pltpu.VMEM((2, 4 * block, TILE), F32),
            pltpu.VMEM((2, 4 * block, TILE), BF16),
            pltpu.VMEM((2, block, 16, 128), BF16),
            pltpu.SemaphoreType.DMA((3, 2)),
            pltpu.SemaphoreType.DMA((3, 2)),
            pltpu.SemaphoreType.DMA((3, 2)),
            pltpu.SemaphoreType.DMA((3, 2)),
            pltpu.SemaphoreType.DMA((3,)),
            pltpu.SemaphoreType.DMA((3,)),
            pltpu.SemaphoreType.DMA((4,)),
            pltpu.SemaphoreType.DMA((4,)),
            pltpu.SemaphoreType.DMA((2,)),
        ],
        compiler_params=pltpu.CompilerParams(
            collective_id=0, has_side_effects=True, vmem_limit_bytes=48 * 1024 * 1024),
        cost_estimate=pl.CostEstimate(flops=10**10, bytes_accessed=8 * 10**6, transcendentals=10**7),
    )(queries, kv, doc_start.reshape(1, block), block_keep)


def solution(mesh):
    return jax.shard_map(
        local,
        mesh=mesh,
        in_specs=(
            P(("col", "row"), None, None),
            P(("col", "row"), None, None),
            P(("col", "row"), None, None),
            P(("col", "row")),
            P(("col", "row"), None),
        ),
        out_specs=P(("col", "row"), None, None),
        check_vma=False,
    )
```

```python
import functools
import math

import jax
import jax.numpy as jnp
from jax import lax
from jax.experimental import pallas as pl
from jax.experimental.pallas import tpu as pltpu
from jax.sharding import PartitionSpec as P

MASKED = -1e30
STAGES = ((0,), (2,), (1, 3), (5, 4), (6, 7), (8,))
OFFSETS = (1, 3, 2)
X_TRANSIT, Y_TRANSIT = 10, 11
CHUNKS = 9
TILE = 256
F32, BF16 = jnp.float32, jnp.bfloat16


def kernel(rows, cols, q_hbm, kv_ref, start_ref, keep_ref, out_hbm,
           kvbuf, kvs, qraw, meta, qbuf, hot, bias, acc, top, sbuf, wbuf, ostage,
           one_send, one_recv, two_send, two_recv, pass_send, pass_recv,
           mate_send, mate_recv, here):
    block = q_hbm.shape[0]
    per_seg = rows // 2
    ring = per_seg // 2
    row, col = lax.axis_index("row"), lax.axis_index("col")
    core = lax.rem(row, 2)
    other = 1 - core
    place = row // 2
    side = lax.rem(place, 2)
    y = place // 2
    chip = col * per_seg + place
    next_col = lax.rem(col + 1, cols)
    last_col = lax.rem(col + cols - 1, cols)

    def device(seg, at_y, at_side, which):
        return {"row": (at_y * 2 + at_side) * 2 + which, "col": seg}

    mate = device(col, y, side, other)

    def beside(step, which):
        x = lax.rem(side * 2 + lax.rem(col, 2) + step + 4, 4)
        return device(col - lax.rem(col, 2) + lax.rem(x, 2), y, x // 2, which)

    def above(step):
        return device(col, lax.rem(y + step + ring, ring), side, core)

    way = 1 - 2 * core

    def remote(src, dst, send, recv, target):
        return pltpu.make_async_remote_copy(
            src_ref=src, dst_ref=dst, send_sem=send, recv_sem=recv,
            device_id=target, device_id_type=pl.DeviceIdType.MESH)

    def arrived(dst, sem):
        remote(dst, dst, mate_send.at[0], sem, mate).wait_recv()

    barrier = pltpu.get_barrier_semaphore()

    def greet(target):
        pl.semaphore_signal(barrier, inc=1, device_id=target, device_id_type=pl.DeviceIdType.MESH)

    greet(mate)
    for which in (0, 1):
        greet(beside(-way, which))

    @pl.when(col > 0)
    def _():
        for which in (0, 1):
            greet(device(last_col, y, side, which))
            greet(device(last_col, y, 1 - side, which))

    @pl.when(col == 0)
    def _():
        kvbuf[2:4] = jnp.zeros((2,) + kvbuf.shape[1:], BF16)

    greet(above(1))
    greet(above(-1))

    def half(which):
        return pl.ds(pl.multiple_of(which * 16, 16), 16)

    own_q = pltpu.make_async_copy(q_hbm.at[:, half(core), :], qraw.at[core], here.at[0])
    own_q.start()

    for which in (0, 1):
        for h in (0, 1):
            kvs[which, 0, h] = kv_ref[which, 0, h]
            kvs[which, 1, h] = kv_ref[which, 1, h].astype(F32).T.astype(BF16)
    own_kv = pltpu.make_async_copy(kvs.at[core], kvbuf.at[0, core], here.at[1])
    own_kv.start()

    backs = [0, 7 - 6 * side, 8]
    slots = [0, 3 - 2 * side, 2]
    for place_at, offset in enumerate(OFFSETS):
        backs += [2 * offset, 2 * offset - 1 + 2 * side]
        slots += [4 + 2 * place_at, 5 + 2 * place_at]

    own_block = chip * 2 + core
    for i in range(CHUNKS):
        for which in (0, 1):
            number = (chip - backs[i]) * 2 + which
            flag = keep_ref[0, jnp.maximum(number, 0)]
            flag = jnp.where(number == own_block, 1, flag)
            line = i * 2 + which
            meta[core, line:line + 1, :] = jnp.full((1, block), flag, jnp.int32)
    line = 2 * CHUNKS
    meta[core, line:line + 1, :] = start_ref[...]

    pl.semaphore_wait(barrier, jnp.where(col < cols - 1, 9, 5))

    sends = [
        remote(kvs.at[other], kvbuf.at[0, core], mate_send.at[2], mate_recv.at[2], mate),
        remote(meta.at[core], meta.at[core], mate_send.at[0], mate_recv.at[0], mate),
        remote(q_hbm.at[:, half(other), :], qraw.at[core], mate_send.at[1], mate_recv.at[1], mate),
    ]
    for which in (0, 1):
        sends.append(remote(kvs.at[which], kvbuf.at[X_TRANSIT, core],
                            one_send.at[0, which], one_recv.at[0, core],
                            beside(1 - 2 * which, which)))
    onward = []
    for slot, at_side in ((2, side), (3, 1 - side)):
        for which in (0, 1):
            onward.append(remote(kvs.at[which], kvbuf.at[slot, core],
                                 one_send.at[slot - 1, which], one_recv.at[slot - 1, core],
                                 device(next_col, y, at_side, which)))
    for send in sends:
        send.start()

    @pl.when(col < cols - 1)
    def _():
        for send in onward:
            send.start()

    def along(i, cross):
        offset = OFFSETS[i]
        held = y + offset < ring
        source = jnp.where(held, 0, 2) + cross
        to = (Y_TRANSIT if offset == 2 else 4 + 2 * i) + cross
        target = above(way) if offset == 2 else above(1 if offset == 1 else -1)
        return remote(kvbuf.at[source], kvbuf.at[to], two_send.at[i, cross], two_recv.at[i, cross],
                      target)

    pass_x = remote(kvbuf.at[X_TRANSIT], kvbuf.at[1], pass_send.at[0], pass_recv.at[0],
                    beside(way, core))
    pass_y = [remote(kvbuf.at[Y_TRANSIT + cross], kvbuf.at[8 + cross],
                     pass_send.at[1 + cross], pass_recv.at[1 + cross], above(way))
              for cross in (0, 1)]

    group = lax.broadcasted_iota(jnp.int32, hot.shape, 1) // 8
    token = lax.broadcasted_iota(jnp.int32, hot.shape, 0)
    hot[...] = jnp.where(group == token, 1.0, 0.0).astype(BF16)

    def make_bias(t):
        starts = meta[t, 2 * CHUNKS:2 * CHUNKS + 1, :]
        key_off = lax.broadcasted_iota(jnp.int32, (block, block), 0)
        query_pos = (chip * 2 + t) * block + lax.broadcasted_iota(jnp.int32, (block, block), 1)
        for i in range(CHUNKS):
            for which in (0, 1):
                key_pos = ((chip - backs[i]) * 2 + which) * block + key_off
                line = i * 2 + which
                flags = meta[t, line:line + 1, :]
                seen = (flags == 1) & (key_pos >= starts) & (key_pos <= query_pos)
                bias[t, i, which * block:(which + 1) * block, :] = (
                    jnp.where(seen, 0.0, MASKED).astype(BF16))

    def regroup(t):
        def piece(i, _):
            at = pl.ds(pl.multiple_of(i * 64, 64), 64)
            raw = qraw[t, at].astype(F32)
            to = pl.ds(pl.multiple_of(i * 512, 512), 512)
            qbuf[t, 0, :, to] = raw[:, :8, :].reshape(512, 128).T.astype(BF16)
            qbuf[t, 1, :, to] = raw[:, 8:, :].reshape(512, 128).T.astype(BF16)
            return 0
        lax.fori_loop(0, block // 64, piece, 0)

    scale = math.log2(math.e) / math.sqrt(128)
    tiles = block * 8 // TILE

    def run(stage, t):
        first, last = stage == 0, stage == len(STAGES) - 1
        used = STAGES[stage]
        span = len(used) * 2 * block
        ones = jnp.ones((16, span), BF16)
        units = [(r, h) for r in range(tiles) for h in (0, 1)]

        def score(n):
            r, h = units[n]
            at = slice(r * TILE, (r + 1) * TILE)
            rhs = jnp.concatenate([qbuf[t, h, :, at], hot[:, at]], axis=0)
            keys = jnp.concatenate(
                [kvbuf[slots[i], which, 0, h] for i in used for which in (0, 1)], axis=0)
            masks = jnp.concatenate([bias[t, i] for i in used], axis=0)
            scores = jnp.dot(jnp.concatenate([keys, masks], axis=1), rhs,
                             preferred_element_type=F32)
            sbuf[n % 2, :span] = scores
            return jnp.max(scores, axis=0, keepdims=True)

        done = []
        ready = score(0)
        for n, (r, h) in enumerate(units):
            at = slice(r * TILE, (r + 1) * TILE)
            new_top = ready
            if n + 1 < len(units):
                ready = score(n + 1)
            if not first:
                old_top = top[t, h, 0:1, at]
                new_top = jnp.maximum(old_top, new_top)
            wbuf[n % 2, :span] = jnp.exp2(((sbuf[n % 2, :span] - new_top) * scale).astype(BF16))
            values = jnp.concatenate(
                [kvbuf[slots[i], which, 1, h] for i in used for which in (0, 1)], axis=1)
            total = jnp.dot(jnp.concatenate([values, ones], axis=0), wbuf[n % 2, :span],
                            preferred_element_type=F32)
            if not first:
                total = total + acc[t, h, :, at] * jnp.exp2((old_top - new_top) * scale)
            if last:
                result = total[:128] / total[128:129]
                done.append(result.T.reshape(TILE // 8, 8, 128))
                if h == 1:
                    both = jnp.concatenate(done[-2:], axis=1).astype(BF16)
                    ostage[t, r * (TILE // 8):(r + 1) * (TILE // 8)] = both
            else:
                acc[t, h, :, at] = total
                top[t, h, 0:1, at] = new_top

    def run_both(stage, between=None):
        def step(t, _):
            run(stage, t)
            if between is not None:
                @pl.when(t == 0)
                def _():
                    between()
            return 0
        lax.fori_loop(0, 2, step, 0)

    def start_own(early):
        for i in (2, 0, 1):
            held = y + OFFSETS[i] < ring

            @pl.when(held if early else jnp.logical_not(held))
            def _():
                along(i, 0).start()

    def hand_on(cross):
        arrived(kvbuf.at[Y_TRANSIT + cross], two_recv.at[2, cross])
        pass_y[cross].start()

    def before(slot):
        @pl.when(col > 0)
        def _():
            for which in (0, 1):
                arrived(kvbuf.at[slot, which], one_recv.at[slot - 1, which])

    def previous():
        before(2)
        start_own(False)

    make_bias(core)
    own_q.wait()
    regroup(core)
    own_kv.wait()
    arrived(kvbuf.at[0, other], mate_recv.at[2])
    start_own(True)
    arrived(meta.at[other], mate_recv.at[0])
    arrived(qraw.at[other], mate_recv.at[1])
    make_bias(other)
    regroup(other)
    def across():
        for which in (0, 1):
            arrived(kvbuf.at[X_TRANSIT, which], one_recv.at[0, which])
        pass_x.start()

    run_both(0, across)
    previous()
    run_both(1)
    arrived(kvbuf.at[1], pass_recv.at[0])
    before(3)
    for i in (2, 0, 1):
        along(i, 1).start()
    arrived(kvbuf.at[4], two_recv.at[0, 0])
    run_both(2, lambda: hand_on(0))
    hand_on(1)
    arrived(kvbuf.at[6], two_recv.at[1, 0])
    arrived(kvbuf.at[5], two_recv.at[0, 1])
    run_both(3)
    arrived(kvbuf.at[7], two_recv.at[1, 1])
    arrived(kvbuf.at[8], pass_recv.at[1])
    run_both(4)
    arrived(kvbuf.at[9], pass_recv.at[2])

    def finish(t, _):
        t = jnp.where(t == 0, other, core)
        run(5, t)

        @pl.when(t == other)
        def _():
            remote(ostage.at[other], out_hbm.at[:, half(core), :],
                   mate_send.at[3], mate_recv.at[3], mate).start()
        return 0

    lax.fori_loop(0, 2, finish, 0)
    own_out = pltpu.make_async_copy(ostage.at[core], out_hbm.at[:, half(core), :], here.at[0])
    own_out.start()
    for send in sends:
        send.wait_send()

    @pl.when(col < cols - 1)
    def _():
        for send in onward:
            send.wait_send()

    for i in range(3):
        for cross in (0, 1):
            along(i, cross).wait_send()
    pass_x.wait_send()
    for copy in pass_y:
        copy.wait_send()
    own_out.wait()
    remote(ostage.at[other], out_hbm.at[:, half(core), :],
           mate_send.at[3], mate_recv.at[3], mate).wait_send()
    arrived(out_hbm.at[:, half(other), :], mate_recv.at[3])


def local(queries, rotated_key_rows, value_matrix_rows, doc_start, block_keep):
    block = queries.shape[0]
    rows, cols = lax.axis_size("row"), lax.axis_size("col")
    kv = jnp.stack([rotated_key_rows, value_matrix_rows])
    kv = kv.reshape(2, block, 2, 2, 128).transpose(2, 0, 3, 1, 4)
    vmem = pl.BlockSpec(memory_space=pltpu.VMEM)
    hbm = pl.BlockSpec(memory_space=pl.ANY)
    return pl.pallas_call(
        functools.partial(kernel, rows, cols),
        out_shape=jax.ShapeDtypeStruct(queries.shape, BF16),
        in_specs=[hbm, vmem, vmem, pl.BlockSpec(memory_space=pltpu.SMEM)],
        out_specs=hbm,
        scratch_shapes=[
            pltpu.VMEM((13, 2, 2, 2, block, 128), BF16),
            pltpu.VMEM((2, 2, 2, block, 128), BF16),
            pltpu.VMEM((2, block, 16, 128), BF16),
            pltpu.VMEM((2, 24, 128), jnp.int32),
            pltpu.VMEM((2, 2, 128, block * 8), BF16),
            pltpu.VMEM((block, block * 8), BF16),
            pltpu.VMEM((2, CHUNKS, 2 * block, block), BF16),
            pltpu.VMEM((2, 2, 144, block * 8), F32),
            pltpu.VMEM((2, 2, 8, block * 8), F32),
            pltpu.VMEM((2, 4 * block, TILE), F32),
            pltpu.VMEM((2, 4 * block, TILE), BF16),
            pltpu.VMEM((2, block, 16, 128), BF16),
            pltpu.SemaphoreType.DMA((3, 2)),
            pltpu.SemaphoreType.DMA((3, 2)),
            pltpu.SemaphoreType.DMA((3, 2)),
            pltpu.SemaphoreType.DMA((3, 2)),
            pltpu.SemaphoreType.DMA((3,)),
            pltpu.SemaphoreType.DMA((3,)),
            pltpu.SemaphoreType.DMA((4,)),
            pltpu.SemaphoreType.DMA((4,)),
            pltpu.SemaphoreType.DMA((2,)),
        ],
        compiler_params=pltpu.CompilerParams(
            collective_id=0, has_side_effects=True, vmem_limit_bytes=48 * 1024 * 1024),
        cost_estimate=pl.CostEstimate(flops=10**10, bytes_accessed=8 * 10**6, transcendentals=10**7),
    )(queries, kv, doc_start.reshape(1, block), block_keep)


def solution(mesh):
    return jax.shard_map(
        local,
        mesh=mesh,
        in_specs=(
            P(("col", "row"), None, None),
            P(("col", "row"), None, None),
            P(("col", "row"), None, None),
            P(("col", "row")),
            P(("col", "row"), None),
        ),
        out_specs=P(("col", "row"), None, None),
        check_vma=False,
    )
```

```python
import functools
import math

import jax
import jax.numpy as jnp
from jax import lax
from jax.experimental import pallas as pl
from jax.experimental.pallas import tpu as pltpu
from jax.sharding import PartitionSpec as P

MASKED = -1e30
STAGES = ((0,), (2,), (1,), (3, 5), (7, 4), (6, 8))
OFFSETS = (1, 3, 2)
X_TRANSIT, Y_TRANSIT = 10, 11
CHUNKS = 9
TILE = 256
F32, BF16 = jnp.float32, jnp.bfloat16


def kernel(rows, cols, q_hbm, kv_ref, start_ref, keep_ref, out_hbm,
           kvbuf, kvs, qraw, meta, qbuf, hot, bias, acc, top, sbuf, wbuf, ostage,
           one_send, one_recv, two_send, two_recv, pass_send, pass_recv,
           mate_send, mate_recv, here):
    block = q_hbm.shape[0]
    per_seg = rows // 2
    ring = per_seg // 2
    row, col = lax.axis_index("row"), lax.axis_index("col")
    core = lax.rem(row, 2)
    other = 1 - core
    place = row // 2
    side = lax.rem(place, 2)
    y = place // 2
    chip = col * per_seg + place
    next_col = lax.rem(col + 1, cols)
    last_col = lax.rem(col + cols - 1, cols)

    def device(seg, at_y, at_side, which):
        return {"row": (at_y * 2 + at_side) * 2 + which, "col": seg}

    mate = device(col, y, side, other)

    def beside(step, which):
        x = lax.rem(side * 2 + lax.rem(col, 2) + step + 4, 4)
        return device(col - lax.rem(col, 2) + lax.rem(x, 2), y, x // 2, which)

    def above(step):
        return device(col, lax.rem(y + step + ring, ring), side, core)

    way = 1 - 2 * core

    def remote(src, dst, send, recv, target):
        return pltpu.make_async_remote_copy(
            src_ref=src, dst_ref=dst, send_sem=send, recv_sem=recv,
            device_id=target, device_id_type=pl.DeviceIdType.MESH)

    def arrived(dst, sem):
        remote(dst, dst, mate_send.at[0], sem, mate).wait_recv()

    barrier = pltpu.get_barrier_semaphore()

    def greet(target):
        pl.semaphore_signal(barrier, inc=1, device_id=target, device_id_type=pl.DeviceIdType.MESH)

    greet(mate)
    for which in (0, 1):
        greet(beside(-way, which))

    @pl.when(col > 0)
    def _():
        for which in (0, 1):
            greet(device(last_col, y, side, which))
            greet(device(last_col, y, 1 - side, which))

    @pl.when(col == 0)
    def _():
        kvbuf[2:4] = jnp.zeros((2,) + kvbuf.shape[1:], BF16)

    greet(above(1))
    greet(above(-1))

    def half(which):
        return pl.ds(pl.multiple_of(which * 16, 16), 16)

    own_q = pltpu.make_async_copy(q_hbm.at[:, half(core), :], qraw.at[core], here.at[0])
    own_q.start()

    for which in (0, 1):
        for h in (0, 1):
            kvs[which, 0, h] = kv_ref[which, 0, h]
            kvs[which, 1, h] = kv_ref[which, 1, h].astype(F32).T.astype(BF16)
    own_kv = pltpu.make_async_copy(kvs.at[core], kvbuf.at[0, core], here.at[1])
    own_kv.start()

    backs = [0, 7 - 6 * side, 8]
    slots = [0, 3 - 2 * side, 2]
    for place_at, offset in enumerate(OFFSETS):
        backs += [2 * offset, 2 * offset - 1 + 2 * side]
        slots += [4 + 2 * place_at, 5 + 2 * place_at]

    own_block = chip * 2 + core
    for i in range(CHUNKS):
        for which in (0, 1):
            number = (chip - backs[i]) * 2 + which
            flag = keep_ref[0, jnp.maximum(number, 0)]
            flag = jnp.where(number == own_block, 1, flag)
            line = i * 2 + which
            meta[core, line:line + 1, :] = jnp.full((1, block), flag, jnp.int32)
    line = 2 * CHUNKS
    meta[core, line:line + 1, :] = start_ref[...]

    pl.semaphore_wait(barrier, jnp.where(col < cols - 1, 9, 5))

    sends = [
        remote(kvs.at[other], kvbuf.at[0, core], mate_send.at[2], mate_recv.at[2], mate),
        remote(meta.at[core], meta.at[core], mate_send.at[0], mate_recv.at[0], mate),
        remote(q_hbm.at[:, half(other), :], qraw.at[core], mate_send.at[1], mate_recv.at[1], mate),
    ]
    for which in (0, 1):
        sends.append(remote(kvs.at[which], kvbuf.at[X_TRANSIT, core],
                            one_send.at[0, which], one_recv.at[0, core],
                            beside(1 - 2 * which, which)))
    onward = []
    for slot, at_side in ((2, side), (3, 1 - side)):
        for which in (0, 1):
            onward.append(remote(kvs.at[which], kvbuf.at[slot, core],
                                 one_send.at[slot - 1, which], one_recv.at[slot - 1, core],
                                 device(next_col, y, at_side, which)))
    for send in sends:
        send.start()

    @pl.when(col < cols - 1)
    def _():
        for send in onward:
            send.start()

    def along(i, cross):
        offset = OFFSETS[i]
        held = y + offset < ring
        source = jnp.where(held, 0, 2) + cross
        to = (Y_TRANSIT if offset == 2 else 4 + 2 * i) + cross
        target = above(way) if offset == 2 else above(1 if offset == 1 else -1)
        return remote(kvbuf.at[source], kvbuf.at[to], two_send.at[i, cross], two_recv.at[i, cross],
                      target)

    pass_x = remote(kvbuf.at[X_TRANSIT], kvbuf.at[1], pass_send.at[0], pass_recv.at[0],
                    beside(way, core))
    pass_y = [remote(kvbuf.at[Y_TRANSIT + cross], kvbuf.at[8 + cross],
                     pass_send.at[1 + cross], pass_recv.at[1 + cross], above(way))
              for cross in (0, 1)]

    group = lax.broadcasted_iota(jnp.int32, hot.shape, 1) // 8
    token = lax.broadcasted_iota(jnp.int32, hot.shape, 0)
    hot[...] = jnp.where(group == token, 1.0, 0.0).astype(BF16)

    def make_bias(t):
        starts = meta[t, 2 * CHUNKS:2 * CHUNKS + 1, :]
        key_off = lax.broadcasted_iota(jnp.int32, (block, block), 0)
        query_pos = (chip * 2 + t) * block + lax.broadcasted_iota(jnp.int32, (block, block), 1)
        for i in range(CHUNKS):
            for which in (0, 1):
                key_pos = ((chip - backs[i]) * 2 + which) * block + key_off
                line = i * 2 + which
                flags = meta[t, line:line + 1, :]
                seen = (flags == 1) & (key_pos >= starts) & (key_pos <= query_pos)
                bias[t, i, which * block:(which + 1) * block, :] = (
                    jnp.where(seen, 0.0, MASKED).astype(BF16))

    def regroup(t):
        def piece(i, _):
            at = pl.ds(pl.multiple_of(i * 64, 64), 64)
            raw = qraw[t, at].astype(F32)
            to = pl.ds(pl.multiple_of(i * 512, 512), 512)
            qbuf[t, 0, :, to] = raw[:, :8, :].reshape(512, 128).T.astype(BF16)
            qbuf[t, 1, :, to] = raw[:, 8:, :].reshape(512, 128).T.astype(BF16)
            return 0
        lax.fori_loop(0, block // 64, piece, 0)

    scale = math.log2(math.e) / math.sqrt(128)
    tiles = block * 8 // TILE

    def run(stage, t, parts=(0, 1)):
        first, last = stage == 0, stage == len(STAGES) - 1
        used = STAGES[stage]
        span = len(used) * len(parts) * block
        ones = jnp.ones((16, span), BF16)
        units = [(r, h) for r in range(tiles) for h in (0, 1)]

        def score(n):
            r, h = units[n]
            at = slice(r * TILE, (r + 1) * TILE)
            rhs = jnp.concatenate([qbuf[t, h, :, at], hot[:, at]], axis=0)
            keys = jnp.concatenate(
                [kvbuf[slots[i], which, 0, h] for i in used for which in parts], axis=0)
            masks = jnp.concatenate(
                [bias[t, i, which * block:(which + 1) * block] for i in used for which in parts],
                axis=0)
            scores = jnp.dot(jnp.concatenate([keys, masks], axis=1), rhs,
                             preferred_element_type=F32)
            sbuf[n % 2, :span] = scores
            return jnp.max(scores, axis=0, keepdims=True)

        done = []
        ready = score(0)
        for n, (r, h) in enumerate(units):
            at = slice(r * TILE, (r + 1) * TILE)
            new_top = ready
            if n + 1 < len(units):
                ready = score(n + 1)
            if not first:
                old_top = top[t, h, 0:1, at]
                new_top = jnp.maximum(old_top, new_top)
            wbuf[n % 2, :span] = jnp.exp2((sbuf[n % 2, :span] - new_top) * scale).astype(BF16)
            values = jnp.concatenate(
                [kvbuf[slots[i], which, 1, h] for i in used for which in parts], axis=1)
            total = jnp.dot(jnp.concatenate([values, ones], axis=0), wbuf[n % 2, :span],
                            preferred_element_type=F32)
            if not first:
                total = total + acc[t, h, :, at] * jnp.exp2((old_top - new_top) * scale)
            if last:
                result = total[:128] / total[128:129]
                done.append(result.T.reshape(TILE // 8, 8, 128))
                if h == 1:
                    both = jnp.concatenate(done[-2:], axis=1).astype(BF16)
                    ostage[t, r * (TILE // 8):(r + 1) * (TILE // 8)] = both
            else:
                acc[t, h, :, at] = total
                top[t, h, 0:1, at] = new_top

    def run_both(stage, between=None):
        def step(t, _):
            run(stage, t)
            if between is not None:
                @pl.when(t == 0)
                def _():
                    between()
            return 0
        lax.fori_loop(0, 2, step, 0)

    def start_own(early):
        for i in (2, 0, 1):
            held = y + OFFSETS[i] < ring

            @pl.when(held if early else jnp.logical_not(held))
            def _():
                along(i, 0).start()

    def hand_on(cross):
        arrived(kvbuf.at[Y_TRANSIT + cross], two_recv.at[2, cross])
        pass_y[cross].start()

    def before(slot):
        @pl.when(col > 0)
        def _():
            for which in (0, 1):
                arrived(kvbuf.at[slot, which], one_recv.at[slot - 1, which])

    def previous():
        before(2)
        start_own(False)

    make_bias(core)
    own_q.wait()
    regroup(core)
    own_kv.wait()
    arrived(kvbuf.at[0, other], mate_recv.at[2])
    start_own(True)
    arrived(meta.at[other], mate_recv.at[0])
    arrived(qraw.at[other], mate_recv.at[1])
    make_bias(other)
    regroup(other)
    def across():
        for which in (0, 1):
            arrived(kvbuf.at[X_TRANSIT, which], one_recv.at[0, which])
        pass_x.start()

    run(0, 0, (0,))
    across()
    run(0, 1)
    previous()
    run(1, 0)
    run(1, 1, (1,))
    arrived(kvbuf.at[1], pass_recv.at[0])
    before(3)
    for i in (2, 0, 1):
        along(i, 1).start()
    run_both(2)
    hand_on(0)
    for i in (0, 1):
        arrived(kvbuf.at[4 + 2 * i], two_recv.at[i, 0])
    run_both(3, lambda: hand_on(1))
    arrived(kvbuf.at[8], pass_recv.at[1])
    arrived(kvbuf.at[5], two_recv.at[0, 1])
    run_both(4)
    arrived(kvbuf.at[7], two_recv.at[1, 1])
    arrived(kvbuf.at[9], pass_recv.at[2])

    def finish(t, _):
        t = jnp.where(t == 0, other, core)
        run(5, t)

        @pl.when(t == other)
        def _():
            remote(ostage.at[other], out_hbm.at[:, half(core), :],
                   mate_send.at[3], mate_recv.at[3], mate).start()
        return 0

    lax.fori_loop(0, 2, finish, 0)
    own_out = pltpu.make_async_copy(ostage.at[core], out_hbm.at[:, half(core), :], here.at[0])
    own_out.start()
    for send in sends:
        send.wait_send()

    @pl.when(col < cols - 1)
    def _():
        for send in onward:
            send.wait_send()

    for i in range(3):
        for cross in (0, 1):
            along(i, cross).wait_send()
    pass_x.wait_send()
    for copy in pass_y:
        copy.wait_send()
    own_out.wait()
    remote(ostage.at[other], out_hbm.at[:, half(core), :],
           mate_send.at[3], mate_recv.at[3], mate).wait_send()
    arrived(out_hbm.at[:, half(other), :], mate_recv.at[3])


def local(queries, rotated_key_rows, value_matrix_rows, doc_start, block_keep):
    block = queries.shape[0]
    rows, cols = lax.axis_size("row"), lax.axis_size("col")
    kv = jnp.stack([rotated_key_rows, value_matrix_rows])
    kv = kv.reshape(2, block, 2, 2, 128).transpose(2, 0, 3, 1, 4)
    vmem = pl.BlockSpec(memory_space=pltpu.VMEM)
    hbm = pl.BlockSpec(memory_space=pl.ANY)
    return pl.pallas_call(
        functools.partial(kernel, rows, cols),
        out_shape=jax.ShapeDtypeStruct(queries.shape, BF16),
        in_specs=[hbm, vmem, vmem, pl.BlockSpec(memory_space=pltpu.SMEM)],
        out_specs=hbm,
        scratch_shapes=[
            pltpu.VMEM((13, 2, 2, 2, block, 128), BF16),
            pltpu.VMEM((2, 2, 2, block, 128), BF16),
            pltpu.VMEM((2, block, 16, 128), BF16),
            pltpu.VMEM((2, 24, 128), jnp.int32),
            pltpu.VMEM((2, 2, 128, block * 8), BF16),
            pltpu.VMEM((block, block * 8), BF16),
            pltpu.VMEM((2, CHUNKS, 2 * block, block), BF16),
            pltpu.VMEM((2, 2, 144, block * 8), F32),
            pltpu.VMEM((2, 2, 8, block * 8), F32),
            pltpu.VMEM((2, 4 * block, TILE), F32),
            pltpu.VMEM((2, 4 * block, TILE), BF16),
            pltpu.VMEM((2, block, 16, 128), BF16),
            pltpu.SemaphoreType.DMA((3, 2)),
            pltpu.SemaphoreType.DMA((3, 2)),
            pltpu.SemaphoreType.DMA((3, 2)),
            pltpu.SemaphoreType.DMA((3, 2)),
            pltpu.SemaphoreType.DMA((3,)),
            pltpu.SemaphoreType.DMA((3,)),
            pltpu.SemaphoreType.DMA((4,)),
            pltpu.SemaphoreType.DMA((4,)),
            pltpu.SemaphoreType.DMA((2,)),
        ],
        compiler_params=pltpu.CompilerParams(
            collective_id=0, has_side_effects=True, vmem_limit_bytes=48 * 1024 * 1024),
        cost_estimate=pl.CostEstimate(flops=10**10, bytes_accessed=8 * 10**6, transcendentals=10**7),
    )(queries, kv, doc_start.reshape(1, block), block_keep)


def solution(mesh):
    return jax.shard_map(
        local,
        mesh=mesh,
        in_specs=(
            P(("col", "row"), None, None),
            P(("col", "row"), None, None),
            P(("col", "row"), None, None),
            P(("col", "row")),
            P(("col", "row"), None),
        ),
        out_specs=P(("col", "row"), None, None),
        check_vma=False,
    )
```

```python
import functools
import math

import jax
import jax.numpy as jnp
from jax import lax
from jax.experimental import pallas as pl
from jax.experimental.pallas import tpu as pltpu
from jax.sharding import PartitionSpec as P

MASKED = -1e30
STAGES = ((0,), (2,), (1,), (3, 5), (7, 4), (6, 8))
OFFSETS = (1, 3, 2)
X_TRANSIT, Y_TRANSIT = 10, 11
CHUNKS = 9
TILE = 256
F32, BF16 = jnp.float32, jnp.bfloat16


def kernel(rows, cols, q_hbm, kv_ref, start_ref, keep_ref, out_hbm,
           kvbuf, kvs, qraw, meta, qbuf, hot, bias, acc, top, sbuf, wbuf, ostage,
           one_send, one_recv, two_send, two_recv, pass_send, pass_recv,
           mate_send, mate_recv, here):
    block = q_hbm.shape[0]
    per_seg = rows // 2
    ring = per_seg // 2
    row, col = lax.axis_index("row"), lax.axis_index("col")
    core = lax.rem(row, 2)
    other = 1 - core
    place = row // 2
    side = lax.rem(place, 2)
    y = place // 2
    chip = col * per_seg + place
    next_col = lax.rem(col + 1, cols)
    last_col = lax.rem(col + cols - 1, cols)

    def device(seg, at_y, at_side, which):
        return {"row": (at_y * 2 + at_side) * 2 + which, "col": seg}

    mate = device(col, y, side, other)

    def beside(step, which):
        x = lax.rem(side * 2 + lax.rem(col, 2) + step + 4, 4)
        return device(col - lax.rem(col, 2) + lax.rem(x, 2), y, x // 2, which)

    def above(step):
        return device(col, lax.rem(y + step + ring, ring), side, core)

    way = 1 - 2 * core

    def remote(src, dst, send, recv, target):
        return pltpu.make_async_remote_copy(
            src_ref=src, dst_ref=dst, send_sem=send, recv_sem=recv,
            device_id=target, device_id_type=pl.DeviceIdType.MESH)

    def arrived(dst, sem):
        remote(dst, dst, mate_send.at[0], sem, mate).wait_recv()

    barrier = pltpu.get_barrier_semaphore()

    def greet(target):
        pl.semaphore_signal(barrier, inc=1, device_id=target, device_id_type=pl.DeviceIdType.MESH)

    greet(mate)
    for which in (0, 1):
        greet(beside(-way, which))

    @pl.when(col > 0)
    def _():
        for which in (0, 1):
            greet(device(last_col, y, side, which))
            greet(device(last_col, y, 1 - side, which))

    @pl.when(col == 0)
    def _():
        kvbuf[2:4] = jnp.zeros((2,) + kvbuf.shape[1:], BF16)

    greet(above(1))
    greet(above(-1))

    def half(which):
        return pl.ds(pl.multiple_of(which * 16, 16), 16)

    own_q = pltpu.make_async_copy(q_hbm.at[:, half(core), :], qraw.at[core], here.at[0])
    own_q.start()

    for which in (0, 1):
        for h in (0, 1):
            kvs[which, 0, h] = kv_ref[which, 0, h]
            kvs[which, 1, h] = kv_ref[which, 1, h].astype(F32).T.astype(BF16)
    own_kv = pltpu.make_async_copy(kvs.at[core], kvbuf.at[0, core], here.at[1])
    own_kv.start()

    backs = [0, 7 - 6 * side, 8]
    slots = [0, 3 - 2 * side, 2]
    for place_at, offset in enumerate(OFFSETS):
        backs += [2 * offset, 2 * offset - 1 + 2 * side]
        slots += [4 + 2 * place_at, 5 + 2 * place_at]

    own_block = chip * 2 + core
    for i in range(CHUNKS):
        for which in (0, 1):
            number = (chip - backs[i]) * 2 + which
            flag = keep_ref[0, jnp.maximum(number, 0)]
            flag = jnp.where(number == own_block, 1, flag)
            line = i * 2 + which
            meta[core, line:line + 1, :] = jnp.full((1, block), flag, jnp.int32)
    line = 2 * CHUNKS
    meta[core, line:line + 1, :] = start_ref[...]

    pl.semaphore_wait(barrier, jnp.where(col < cols - 1, 9, 5))

    sends = [
        remote(kvs.at[other], kvbuf.at[0, core], mate_send.at[2], mate_recv.at[2], mate),
        remote(meta.at[core], meta.at[core], mate_send.at[0], mate_recv.at[0], mate),
        remote(q_hbm.at[:, half(other), :], qraw.at[core], mate_send.at[1], mate_recv.at[1], mate),
    ]
    for which in (0, 1):
        sends.append(remote(kvs.at[which], kvbuf.at[X_TRANSIT, core],
                            one_send.at[0, which], one_recv.at[0, core],
                            beside(1 - 2 * which, which)))
    onward = []
    for slot, at_side in ((2, side), (3, 1 - side)):
        for which in (0, 1):
            onward.append(remote(kvs.at[which], kvbuf.at[slot, core],
                                 one_send.at[slot - 1, which], one_recv.at[slot - 1, core],
                                 device(next_col, y, at_side, which)))
    for number in (3, 4, 0, 1):
        sends[number].start()

    @pl.when(col < cols - 1)
    def _():
        for send in onward[:2]:
            send.start()

    sends[2].start()

    @pl.when(col < cols - 1)
    def _():
        for send in onward[2:]:
            send.start()

    def along(i, cross):
        offset = OFFSETS[i]
        held = y + offset < ring
        source = jnp.where(held, 0, 2) + cross
        to = (Y_TRANSIT if offset == 2 else 4 + 2 * i) + cross
        target = above(way) if offset == 2 else above(1 if offset == 1 else -1)
        return remote(kvbuf.at[source], kvbuf.at[to], two_send.at[i, cross], two_recv.at[i, cross],
                      target)

    pass_x = remote(kvbuf.at[X_TRANSIT], kvbuf.at[1], pass_send.at[0], pass_recv.at[0],
                    beside(way, core))
    pass_y = [remote(kvbuf.at[Y_TRANSIT + cross], kvbuf.at[8 + cross],
                     pass_send.at[1 + cross], pass_recv.at[1 + cross], above(way))
              for cross in (0, 1)]

    group = lax.broadcasted_iota(jnp.int32, hot.shape, 1) // 8
    token = lax.broadcasted_iota(jnp.int32, hot.shape, 0)
    hot[...] = jnp.where(group == token, 1.0, 0.0).astype(BF16)

    def make_bias(t):
        starts = meta[t, 2 * CHUNKS:2 * CHUNKS + 1, :]
        key_off = lax.broadcasted_iota(jnp.int32, (block, block), 0)
        query_pos = (chip * 2 + t) * block + lax.broadcasted_iota(jnp.int32, (block, block), 1)
        for i in range(CHUNKS):
            for which in (0, 1):
                key_pos = ((chip - backs[i]) * 2 + which) * block + key_off
                line = i * 2 + which
                flags = meta[t, line:line + 1, :]
                seen = (flags == 1) & (key_pos >= starts) & (key_pos <= query_pos)
                bias[t, i, which * block:(which + 1) * block, :] = (
                    jnp.where(seen, 0.0, MASKED).astype(BF16))

    def regroup(t):
        def piece(i, _):
            at = pl.ds(pl.multiple_of(i * 64, 64), 64)
            raw = qraw[t, at].astype(F32)
            to = pl.ds(pl.multiple_of(i * 512, 512), 512)
            qbuf[t, 0, :, to] = raw[:, :8, :].reshape(512, 128).T.astype(BF16)
            qbuf[t, 1, :, to] = raw[:, 8:, :].reshape(512, 128).T.astype(BF16)
            return 0
        lax.fori_loop(0, block // 64, piece, 0)

    scale = math.log2(math.e) / math.sqrt(128)
    tiles = block * 8 // TILE

    def run(stage, t, parts=(0, 1)):
        first, last = stage == 0, stage == len(STAGES) - 1
        used = STAGES[stage]
        span = len(used) * len(parts) * block
        ones = jnp.ones((16, span), BF16)
        units = [(r, h) for r in range(tiles) for h in (0, 1)]

        def score(n):
            r, h = units[n]
            at = slice(r * TILE, (r + 1) * TILE)
            rhs = jnp.concatenate([qbuf[t, h, :, at], hot[:, at]], axis=0)
            keys = jnp.concatenate(
                [kvbuf[slots[i], which, 0, h] for i in used for which in parts], axis=0)
            masks = jnp.concatenate(
                [bias[t, i, which * block:(which + 1) * block] for i in used for which in parts],
                axis=0)
            scores = jnp.dot(jnp.concatenate([keys, masks], axis=1), rhs,
                             preferred_element_type=F32)
            sbuf[n % 2, :span] = scores
            return jnp.max(scores, axis=0, keepdims=True)

        done = []
        ready = score(0)
        for n, (r, h) in enumerate(units):
            at = slice(r * TILE, (r + 1) * TILE)
            new_top = ready
            if n + 1 < len(units):
                ready = score(n + 1)
            if not first:
                old_top = top[t, h, 0:1, at]
                new_top = jnp.maximum(old_top, new_top)
            wbuf[n % 2, :span] = jnp.exp2((sbuf[n % 2, :span] - new_top) * scale).astype(BF16)
            values = jnp.concatenate(
                [kvbuf[slots[i], which, 1, h] for i in used for which in parts], axis=1)
            total = jnp.dot(jnp.concatenate([values, ones], axis=0), wbuf[n % 2, :span],
                            preferred_element_type=F32)
            if not first:
                total = total + acc[t, h, :, at] * jnp.exp2((old_top - new_top) * scale)
            if last:
                result = total[:128] / total[128:129]
                done.append(result.T.reshape(TILE // 8, 8, 128))
                if h == 1:
                    both = jnp.concatenate(done[-2:], axis=1).astype(BF16)
                    ostage[t, r * (TILE // 8):(r + 1) * (TILE // 8)] = both
            else:
                acc[t, h, :, at] = total
                top[t, h, 0:1, at] = new_top

    def run_both(stage, between=None):
        def step(t, _):
            run(stage, t)
            if between is not None:
                @pl.when(t == 0)
                def _():
                    between()
            return 0
        lax.fori_loop(0, 2, step, 0)

    def start_own(early):
        for i in (2, 0, 1):
            held = y + OFFSETS[i] < ring

            @pl.when(held if early else jnp.logical_not(held))
            def _():
                along(i, 0).start()

    def hand_on(cross):
        arrived(kvbuf.at[Y_TRANSIT + cross], two_recv.at[2, cross])
        pass_y[cross].start()

    def before(slot):
        @pl.when(col > 0)
        def _():
            for which in (0, 1):
                arrived(kvbuf.at[slot, which], one_recv.at[slot - 1, which])

    def previous():
        before(2)
        start_own(False)

    make_bias(core)
    own_q.wait()
    regroup(core)
    own_kv.wait()
    arrived(kvbuf.at[0, other], mate_recv.at[2])
    start_own(True)
    arrived(meta.at[other], mate_recv.at[0])
    arrived(qraw.at[other], mate_recv.at[1])
    make_bias(other)
    regroup(other)
    def across():
        for which in (0, 1):
            arrived(kvbuf.at[X_TRANSIT, which], one_recv.at[0, which])
        pass_x.start()

    run(0, 0, (0,))
    across()
    run(0, 1)
    previous()
    run(1, 0)
    run(1, 1, (1,))
    arrived(kvbuf.at[1], pass_recv.at[0])
    before(3)
    for i in (2, 0, 1):
        along(i, 1).start()
    run_both(2)
    hand_on(0)
    for i in (0, 1):
        arrived(kvbuf.at[4 + 2 * i], two_recv.at[i, 0])
    run_both(3, lambda: hand_on(1))
    arrived(kvbuf.at[8], pass_recv.at[1])
    arrived(kvbuf.at[5], two_recv.at[0, 1])
    run_both(4)
    arrived(kvbuf.at[7], two_recv.at[1, 1])
    arrived(kvbuf.at[9], pass_recv.at[2])

    def finish(t, _):
        t = jnp.where(t == 0, other, core)
        run(5, t)

        @pl.when(t == other)
        def _():
            remote(ostage.at[other], out_hbm.at[:, half(core), :],
                   mate_send.at[3], mate_recv.at[3], mate).start()
        return 0

    lax.fori_loop(0, 2, finish, 0)
    own_out = pltpu.make_async_copy(ostage.at[core], out_hbm.at[:, half(core), :], here.at[0])
    own_out.start()
    for send in sends:
        send.wait_send()

    @pl.when(col < cols - 1)
    def _():
        for send in onward:
            send.wait_send()

    for i in range(3):
        for cross in (0, 1):
            along(i, cross).wait_send()
    pass_x.wait_send()
    for copy in pass_y:
        copy.wait_send()
    own_out.wait()
    remote(ostage.at[other], out_hbm.at[:, half(core), :],
           mate_send.at[3], mate_recv.at[3], mate).wait_send()
    arrived(out_hbm.at[:, half(other), :], mate_recv.at[3])


def local(queries, rotated_key_rows, value_matrix_rows, doc_start, block_keep):
    block = queries.shape[0]
    rows, cols = lax.axis_size("row"), lax.axis_size("col")
    kv = jnp.stack([rotated_key_rows, value_matrix_rows])
    kv = kv.reshape(2, block, 2, 2, 128).transpose(2, 0, 3, 1, 4)
    vmem = pl.BlockSpec(memory_space=pltpu.VMEM)
    hbm = pl.BlockSpec(memory_space=pl.ANY)
    return pl.pallas_call(
        functools.partial(kernel, rows, cols),
        out_shape=jax.ShapeDtypeStruct(queries.shape, BF16),
        in_specs=[hbm, vmem, vmem, pl.BlockSpec(memory_space=pltpu.SMEM)],
        out_specs=hbm,
        scratch_shapes=[
            pltpu.VMEM((13, 2, 2, 2, block, 128), BF16),
            pltpu.VMEM((2, 2, 2, block, 128), BF16),
            pltpu.VMEM((2, block, 16, 128), BF16),
            pltpu.VMEM((2, 24, 128), jnp.int32),
            pltpu.VMEM((2, 2, 128, block * 8), BF16),
            pltpu.VMEM((block, block * 8), BF16),
            pltpu.VMEM((2, CHUNKS, 2 * block, block), BF16),
            pltpu.VMEM((2, 2, 144, block * 8), F32),
            pltpu.VMEM((2, 2, 8, block * 8), F32),
            pltpu.VMEM((2, 4 * block, TILE), F32),
            pltpu.VMEM((2, 4 * block, TILE), BF16),
            pltpu.VMEM((2, block, 16, 128), BF16),
            pltpu.SemaphoreType.DMA((3, 2)),
            pltpu.SemaphoreType.DMA((3, 2)),
            pltpu.SemaphoreType.DMA((3, 2)),
            pltpu.SemaphoreType.DMA((3, 2)),
            pltpu.SemaphoreType.DMA((3,)),
            pltpu.SemaphoreType.DMA((3,)),
            pltpu.SemaphoreType.DMA((4,)),
            pltpu.SemaphoreType.DMA((4,)),
            pltpu.SemaphoreType.DMA((2,)),
        ],
        compiler_params=pltpu.CompilerParams(
            collective_id=0, has_side_effects=True, vmem_limit_bytes=48 * 1024 * 1024),
        cost_estimate=pl.CostEstimate(flops=10**10, bytes_accessed=8 * 10**6, transcendentals=10**7),
    )(queries, kv, doc_start.reshape(1, block), block_keep)


def solution(mesh):
    return jax.shard_map(
        local,
        mesh=mesh,
        in_specs=(
            P(("col", "row"), None, None),
            P(("col", "row"), None, None),
            P(("col", "row"), None, None),
            P(("col", "row")),
            P(("col", "row"), None),
        ),
        out_specs=P(("col", "row"), None, None),
        check_vma=False,
    )
```
